128 devices in a mesh: vol: 8 (over z, core), ctl: 16 (over y, x).
Axes of the slice: x: 4, y: 4, z: 4, core: 2. Of those that a mesh axis runs over, the one named last changes fastest.
Arguments:
- sensitivity: float32 [3, 262144], P(None, ('vol', 'ctl')), may hold values from -24 to 24
- sens_ids: int32 [2048], P(('vol', 'ctl')), may hold values from 0 to 2047
- ctl_coords: float32 [3, 262144], P(None, 'ctl'), may hold values from -87 to 87
- partners: int32 [2048, 8], P('ctl'), may hold values from 0 to 2047, as said below
- node_coords: float32 [3, 1048576], P(None, ('vol', 'ctl')), may hold values from -87 to 87
- node_tiles: int32 [8192, 9], P(('vol', 'ctl')), may hold values from 0 to 2047, as said below
Outputs:
- control_weights: float32 [3, 262144], P(None, 'ctl')
- node_shift: float32 [3, 1048576], P(None, ('vol', 'ctl'))
The draws below stay inside these ranges and needn't reach their ends.
Inputs may be any that keep to these rules, and one draw needn't show every extreme that they name: In each column the partners pair up the control blocks: if block b names block e, then e names b in the same column, and no block names itself. `node_tiles`: the 9 blocks of a row are distinct.
All inputs are finite; a program needn't handle non-finite values.
Results may differ from the reference program's by a relative error of at most 0.0003.
Values sent between devices are 32-bit elements; how exact they have to be, the bound alone decides.
No kernel may reach another device: no remote copies, remote signals or barrier semaphores. Data moves between devices by JAX's collectives and lax.ppermute only.
A program may use at most 64 MiB of HBM per device.

```python
import math
import jax
import jax.numpy as jnp
from jax import lax

BS = 128
ITERS = 2
CBLK_DEV = 128
NBLK_DEV = 64
NCB = 2048
NC = 262144
SBLK = 2048
NBT = 8192
NN = 1048576


def sens_layout(key):
    owners = jax.random.randint(jax.random.fold_in(key, 11), (SBLK,), 0, NCB).astype(jnp.int32)
    owners = owners.at[0].set(NCB - 1)
    owners = owners.at[1].set(0)
    return owners


def draw_sens_ids(key, part):
    return sens_layout(key)


def draw_sensitivity(key, part):
    owners = sens_layout(key)
    rise = 1.0 + 2.0 * owners.astype(jnp.float32) / (NCB - 1)
    noise_key = jax.random.fold_in(key, 12)
    level_key = jax.random.fold_in(key, 13)
    base = jnp.clip(jax.random.normal(noise_key, (3, SBLK, BS), jnp.float32), -6.0, 6.0)
    level = jnp.exp(jax.random.uniform(level_key, (SBLK,), jnp.float32, 0.0, math.log(4.0)))
    values = 0.3 * base * (level * rise)[None, :, None]
    return values.reshape(3, SBLK * BS).astype(jnp.float32)


def cell_layout(key):
    cell_of = jax.random.permutation(jax.random.fold_in(key, 31), NCB).astype(jnp.int32)
    block_of = jnp.zeros((NCB,), jnp.int32).at[cell_of].set(jnp.arange(NCB, dtype=jnp.int32))
    return (cell_of, block_of)


def flip_next(position, period):
    return jnp.mod((position + 1 ^ 1) - 1, period).astype(jnp.int32)


def draw_partners(key, part):
    cell_of, block_of = cell_layout(key)
    beside_all = NCB // 4
    sector = cell_of // 4
    axial = cell_of % 4
    sector_pair = sector ^ 1
    sector_next = flip_next(sector, beside_all)
    axial_pair = axial ^ 1
    axial_next = flip_next(axial, 4)
    mate_list = [(sector_pair, axial), (sector_next, axial), (sector, axial_pair), (sector, axial_next), (sector_pair, axial_pair), (sector_pair, axial_next), (sector_next, axial_pair), (sector_next, axial_next)]
    columns = [block_of[pair[0] * 4 + pair[1]] for pair in mate_list]
    return jnp.stack(columns, axis=1).astype(jnp.int32)


def draw_ctl_coords(key, part):
    cell_of, block_of = cell_layout(key)
    beside_all = NCB // 4
    radius = beside_all / (2.0 * math.pi)
    sector = (cell_of // 4).astype(jnp.float32)[:, None]
    axial = (cell_of % 4).astype(jnp.float32)[:, None]
    along = jax.random.uniform(jax.random.fold_in(key, 32), (NCB, BS), jnp.float32)
    upward = jax.random.uniform(jax.random.fold_in(key, 33), (NCB, BS), jnp.float32)
    depth = jax.random.uniform(jax.random.fold_in(key, 34), (NCB, BS), jnp.float32)
    theta = 2.0 * math.pi * (sector + along) / beside_all
    spoke = radius - 0.1 * depth
    coords = jnp.stack([spoke * jnp.cos(theta), spoke * jnp.sin(theta), axial + upward])
    return coords.reshape(3, NC).astype(jnp.float32)


def node_layout(key):
    cell_of, block_of = cell_layout(key)
    beside_all = NCB // 4
    sector = jax.random.randint(jax.random.fold_in(key, 41), (NBT,), 0, beside_all).astype(jnp.int32)
    axial = jax.random.randint(jax.random.fold_in(key, 42), (NBT,), 1, 3).astype(jnp.int32)
    last_cell = cell_of[NCB - 1]
    first_cell = cell_of[0]
    sector = sector.at[0].set(last_cell // 4).at[1].set(first_cell // 4)
    axial = axial.at[0].set(jnp.clip(last_cell % 4, 1, 2)).at[1].set(jnp.clip(first_cell % 4, 1, 2))
    return (sector, axial, block_of)


def draw_node_tiles(key, part):
    sector, axial, block_of = node_layout(key)
    beside_all = NCB // 4
    columns = []
    for step_sector in (-1, 0, 1):
        for step_axial in (-1, 0, 1):
            cell = jnp.mod(sector + step_sector, beside_all) * 4 + axial + step_axial
            columns.append(block_of[cell])
    return jnp.stack(columns, axis=1).astype(jnp.int32)


def draw_node_coords(key, part):
    sector, axial, block_of = node_layout(key)
    beside_all = NCB // 4
    radius = beside_all / (2.0 * math.pi)
    along = jax.random.uniform(jax.random.fold_in(key, 43), (NBT, BS), jnp.float32)
    upward = jax.random.uniform(jax.random.fold_in(key, 44), (NBT, BS), jnp.float32)
    lift = jax.random.uniform(jax.random.fold_in(key, 45), (NBT, BS), jnp.float32)
    theta = 2.0 * math.pi * (sector.astype(jnp.float32)[:, None] + along) / beside_all
    spoke = radius + 0.5 * lift
    coords = jnp.stack([spoke * jnp.cos(theta), spoke * jnp.sin(theta), axial.astype(jnp.float32)[:, None] + upward])
    return coords.reshape(3, NN).astype(jnp.float32)


def setup_inputs(seed: int = 0) -> dict:
    key_of = jax.random.split(jax.random.key(seed), 7)
    return {
        "sensitivity": draw_sensitivity(jax.random.fold_in(key_of[6], 71), 0),
        "sens_ids": draw_sens_ids(jax.random.fold_in(key_of[6], 71), 0),
        "ctl_coords": draw_ctl_coords(jax.random.fold_in(key_of[6], 71), 0),
        "partners": draw_partners(jax.random.fold_in(key_of[6], 71), 0),
        "node_coords": draw_node_coords(jax.random.fold_in(key_of[6], 71), 0),
        "node_tiles": draw_node_tiles(jax.random.fold_in(key_of[6], 71), 0),
    }


highest = lax.Precision.HIGHEST
coupling = 0.0625
node_scale = 0.25

def wendland(dist_sq):
    ratio = jnp.sqrt(dist_sq)
    inner = jnp.maximum(1.0 - ratio, 0.0)
    return inner * inner * inner * inner * (4.0 * ratio + 1.0)

def squared_gap(left, right):
    first = left[0] - right[0]
    second = left[1] - right[1]
    third = left[2] - right[2]
    return first * first + second * second + third * third

def block_apply(vec_part, pts_part, mate_pts, mate_vec, mates):
    self_tile = wendland(squared_gap(pts_part[:, :, :, None], pts_part[:, :, None, :]))
    mate_tile = wendland(squared_gap(pts_part[:, :, None, :, None], mate_pts[:, :, :, None, :]))
    near = jnp.einsum('kij,ckj->cki', self_tile, vec_part, precision=highest)
    far = jnp.einsum('khij,ckhj->cki', mate_tile, mate_vec, precision=highest)
    return vec_part + (mates * near + far) * coupling

def operator_apply(vec, pts, partners):
    mates = partners.shape[1]
    groups = NCB // CBLK_DEV

    def split_groups(array):
        return array.reshape(3, groups, CBLK_DEV, BS).transpose(1, 0, 2, 3)

    def one_group(args):
        vec_part, pts_part, lists = args
        mate_pts = jnp.take(pts, lists, axis=1)
        mate_vec = jnp.take(vec, lists, axis=1)
        return block_apply(vec_part, pts_part, mate_pts, mate_vec, mates)
    out = lax.map(one_group, (split_groups(vec), split_groups(pts), partners.reshape(groups, CBLK_DEV, mates)))
    return out.transpose(1, 0, 2, 3).reshape(3, NCB, BS)

def reference(sensitivity, sens_ids, ctl_coords, partners, node_coords, node_tiles):
    sens_blocks = sensitivity.reshape(3, SBLK, BS)

    def seg(values):
        return jax.ops.segment_sum(values, sens_ids, num_segments=NCB)
    forcing = jax.vmap(seg)(sens_blocks)
    pts = ctl_coords.reshape(3, NCB, BS)
    weights = jnp.zeros_like(forcing)
    residual = forcing
    direction = forcing
    norm_now = lax.optimization_barrier(jnp.sum(residual * residual, axis=(1, 2)))
    for step in range(ITERS):
        image = operator_apply(direction, pts, partners)
        alpha = norm_now / lax.optimization_barrier(jnp.sum(direction * image, axis=(1, 2)))
        weights = weights + alpha[:, None, None] * direction
        residual = residual - alpha[:, None, None] * image
        norm_next = lax.optimization_barrier(jnp.sum(residual * residual, axis=(1, 2)))
        direction = residual + (norm_next / norm_now)[:, None, None] * direction
        norm_now = norm_next
    reach = node_tiles.shape[1]
    groups = NBT // NBLK_DEV

    def shift_group(args):
        node_part, lists = args
        near_pts = jnp.take(pts, lists, axis=1)
        near_w = jnp.take(weights, lists, axis=1)
        tile = wendland(squared_gap(node_part[:, :, None, :, None], near_pts[:, :, :, None, :]))
        return jnp.einsum('gtij,cgtj->cgi', tile, near_w, precision=highest) * node_scale
    node_groups = node_coords.reshape(3, groups, NBLK_DEV, BS).transpose(1, 0, 2, 3)
    shifted = lax.map(shift_group, (node_groups, node_tiles.reshape(groups, NBLK_DEV, reach)))
    node_shift = shifted.transpose(1, 0, 2, 3).reshape(3, NN)
    return (weights.reshape(3, NC), node_shift)
```

```python
import functools

import jax
import jax.numpy as jnp
from jax import lax
from jax.experimental import pallas as pl
from jax.experimental.pallas import tpu as pltpu
from jax.sharding import PartitionSpec as P

BS = 128
COUPLING = 0.0625
NODE_SCALE = 0.25
VMEM = 56 * 1024 * 1024
CHUNK = 32


def whole(shape):
    return pl.BlockSpec(shape, lambda *a: (0,) * len(shape))


def lane_sums(acc):
    ones = jnp.ones((8, BS), jnp.bfloat16)
    dims = (((1,), (1,)), ((), ()))
    rows = lax.broadcasted_iota(jnp.int32, (8, BS), 0)
    out = jnp.zeros((8, BS), jnp.float32)
    for k, part in enumerate(acc):
        high = part.astype(jnp.bfloat16)
        rest = part - high.astype(jnp.float32)
        mid = rest.astype(jnp.bfloat16)
        total = lax.dot_general(ones, high, dims, preferred_element_type=jnp.float32)
        total = total + lax.dot_general(ones, mid, dims, preferred_element_type=jnp.float32)
        out = jnp.where(rows == k, total, out)
    return out


def tiles_kernel(reach, group, with_vec, idx_ref, pts_ref, ctl_ref, *refs):
    if with_vec:
        vec_ref, tile_ref, sum_ref, acc_ref = refs
    else:
        (tile_ref,) = refs
    step = pl.program_id(0)

    def one(g, carry):
        cols = jnp.transpose(pts_ref[g])
        base = (step * group + g) * reach
        for lo in range(0, BS, CHUNK):
            own = [jnp.broadcast_to(cols[lo : lo + CHUNK, k : k + 1], (CHUNK, BS)) for k in range(3)]
            acc = [jnp.zeros((CHUNK, BS), jnp.float32) for _ in range(3)]
            for t in range(reach):
                at = idx_ref[base + t]
                dist = None
                for k in range(3):
                    gap = own[k] - ctl_ref[pl.ds(at + 16 * k, 1), :]
                    dist = gap * gap if dist is None else dist + gap * gap
                ratio = dist * lax.rsqrt(jnp.maximum(dist, 1e-30))
                inner = jnp.maximum(1.0 - ratio, 0.0)
                sq = inner * inner
                tile = (sq * sq) * (4.0 * ratio + 1.0)
                tile_ref[g * reach + t, lo : lo + CHUNK, :] = tile
                if with_vec:
                    for k in range(3):
                        acc[k] = acc[k] + tile * vec_ref[pl.ds(at + 16 * k, 1), :]
            if with_vec:
                for k in range(3):
                    acc_ref[k, lo : lo + CHUNK, :] = acc[k]
        if with_vec:
            sum_ref[g] = lane_sums([acc_ref[k] for k in range(3)])
        return carry

    lax.fori_loop(0, group, one, 0)


def make_tiles(idx, pts, ctl, vec, reach, group):
    count = pts.shape[0]
    with_vec = vec is not None
    out_shape = [jax.ShapeDtypeStruct((count * reach, BS, BS), jnp.float32)]
    out_specs = [pl.BlockSpec((group * reach, BS, BS), lambda m, *_: (m, 0, 0))]
    scratch = []
    operands = [pts, ctl]
    in_specs = [pl.BlockSpec((group, 8, BS), lambda m, *_: (m, 0, 0)), whole(ctl.shape)]
    if with_vec:
        out_shape.append(jax.ShapeDtypeStruct((count, 8, BS), jnp.float32))
        out_specs.append(pl.BlockSpec((group, 8, BS), lambda m, *_: (m, 0, 0)))
        scratch = [pltpu.VMEM((3, BS, BS), jnp.float32)]
        operands.append(vec)
        in_specs.append(whole(vec.shape))
    elements = count * reach * BS * BS
    return pl.pallas_call(
        functools.partial(tiles_kernel, reach, group, with_vec),
        out_shape=out_shape,
        grid_spec=pltpu.PrefetchScalarGridSpec(
            num_scalar_prefetch=1,
            grid=(count // group,),
            in_specs=in_specs,
            out_specs=out_specs,
            scratch_shapes=scratch,
        ),
        compiler_params=pltpu.CompilerParams(vmem_limit_bytes=VMEM),
        cost_estimate=pl.CostEstimate(
            flops=elements * 24, bytes_accessed=elements * 4, transcendentals=elements
        ),
    )(idx, *operands)


def apply_kernel(reach, group, stride, first_scale, idx_ref, tile_ref, vec_ref, sum_ref, acc_ref):
    step = pl.program_id(0)

    def one(g, carry):
        base = (step * group + g) * reach
        for lo in range(0, BS, CHUNK):
            acc = [jnp.zeros((CHUNK, BS), jnp.float32) for _ in range(3)]
            for t in range(reach):
                at = idx_ref[base + t]
                tile = tile_ref[g * reach + t, lo : lo + CHUNK, :]
                for k in range(3):
                    row = vec_ref[pl.ds(at + stride * k, 1), :]
                    if t == 0 and first_scale != 1.0:
                        row = row * first_scale
                    acc[k] = acc[k] + tile * row
            for k in range(3):
                acc_ref[k, lo : lo + CHUNK, :] = acc[k]
        sum_ref[g] = lane_sums([acc_ref[k] for k in range(3)])
        return carry

    lax.fori_loop(0, group, one, 0)


def apply_tiles(idx, tiles, vec, reach, group, stride, first_scale):
    count = tiles.shape[0] // reach
    elements = tiles.size
    return pl.pallas_call(
        functools.partial(apply_kernel, reach, group, stride, first_scale),
        out_shape=jax.ShapeDtypeStruct((count, 8, BS), jnp.float32),
        grid_spec=pltpu.PrefetchScalarGridSpec(
            num_scalar_prefetch=1,
            grid=(count // group,),
            in_specs=[
                pl.BlockSpec((group * reach, BS, BS), lambda m, *_: (m, 0, 0)),
                whole(vec.shape),
            ],
            out_specs=pl.BlockSpec((group, 8, BS), lambda m, *_: (m, 0, 0)),
            scratch_shapes=[pltpu.VMEM((3, BS, BS), jnp.float32)],
        ),
        compiler_params=pltpu.CompilerParams(vmem_limit_bytes=VMEM),
        cost_estimate=pl.CostEstimate(
            flops=elements * 6, bytes_accessed=elements * 4, transcendentals=0
        ),
    )(idx, tiles, vec)


def spread_kernel(rows, want_ref, sens_ref, out_ref):
    ids = jnp.sum(sens_ref[:, 48, :].reshape(16, 8, BS), axis=1)
    want = want_ref[...]
    acc = [jnp.zeros((rows, BS), jnp.float32) for _ in range(3)]
    for g in range(16):
        hot = (want == ids[g : g + 1, :]).astype(jnp.bfloat16)
        for k in range(3):
            part = sens_ref[8 * g : 8 * g + 8, 16 * k : 16 * k + 16, :].reshape(BS, BS)
            for piece in range(3):
                cut = part.astype(jnp.bfloat16)
                acc[k] = acc[k] + jnp.dot(hot, cut, preferred_element_type=jnp.float32)
                if piece < 2:
                    part = part - cut.astype(jnp.float32)
    for k in range(3):
        out_ref[k] = acc[k]


def spread(want, sens):
    rows = want.shape[0]
    return pl.pallas_call(
        functools.partial(spread_kernel, rows),
        out_shape=jax.ShapeDtypeStruct((3, rows, BS), jnp.float32),
        compiler_params=pltpu.CompilerParams(vmem_limit_bytes=VMEM),
        cost_estimate=pl.CostEstimate(
            flops=rows * 2048 * 384 * 6, bytes_accessed=sens.size * 4, transcendentals=0
        ),
    )(want, sens)


def spread_all_kernel(sens_ref, out_ref, cut_ref, ids_ref):
    step = pl.program_id(0)

    @pl.when(step == 0)
    def _():
        ids_ref[...] = jnp.sum(sens_ref[:, 48, :].reshape(16, 8, BS), axis=1)
        for k in range(3):
            part = sens_ref[:, 16 * k : 16 * k + 16, :].reshape(2048, BS)
            high = part.astype(jnp.bfloat16)
            cut_ref[0, :, k * BS : (k + 1) * BS] = high
            cut_ref[1, :, k * BS : (k + 1) * BS] = (part - high.astype(jnp.float32)).astype(jnp.bfloat16)

    want = (lax.broadcasted_iota(jnp.int32, (256, BS), 0) + step * 256).astype(jnp.float32)
    hot = jnp.concatenate(
        [(want == ids_ref[g : g + 1, :]).astype(jnp.bfloat16) for g in range(16)], axis=1
    )
    acc = jnp.dot(hot, cut_ref[0], preferred_element_type=jnp.float32)
    acc = acc + jnp.dot(hot, cut_ref[1], preferred_element_type=jnp.float32)
    for k in range(3):
        out_ref[:, 16 * k : 16 * k + 16, :] = acc[:, k * BS : (k + 1) * BS].reshape(16, 16, BS)


def spread_all(sens):
    return pl.pallas_call(
        spread_all_kernel,
        out_shape=jax.ShapeDtypeStruct((128, 48, BS), jnp.float32),
        grid=(8,),
        in_specs=[whole(sens.shape)],
        out_specs=pl.BlockSpec((16, 48, BS), lambda m: (m, 0, 0)),
        scratch_shapes=[
            pltpu.VMEM((2, 2048, 3 * BS), jnp.bfloat16),
            pltpu.VMEM((16, BS), jnp.float32),
        ],
        compiler_params=pltpu.CompilerParams(vmem_limit_bytes=VMEM),
        cost_estimate=pl.CostEstimate(
            flops=2048 * 2048 * 384 * 4, bytes_accessed=sens.size * 8, transcendentals=0
        ),
    )(sens)


def total_of(part):
    return jnp.sum(jnp.sum(part, axis=0, keepdims=True), axis=1, keepdims=True)


def step_kernel(f_ref, q_ref, p_ref, coef_ref):
    zeros = tuple(jnp.zeros((16, BS), jnp.float32) for _ in range(6))

    def first(d, carry):
        out = []
        for k in range(3):
            f, q = f_ref[d, 16 * k : 16 * k + 16, :], q_ref[d, 16 * k : 16 * k + 16, :]
            out += [carry[2 * k] + f * f, carry[2 * k + 1] + f * q]
        return tuple(out)

    sums = lax.fori_loop(0, 128, first, zeros, unroll=4)
    now = [total_of(sums[2 * k]) for k in range(3)]
    alpha = [now[k] / total_of(sums[2 * k + 1]) for k in range(3)]

    def second(d, carry):
        out = []
        for k in range(3):
            f, q = f_ref[d, 16 * k : 16 * k + 16, :], q_ref[d, 16 * k : 16 * k + 16, :]
            r = f - alpha[k] * q
            p_ref[d, 16 * k : 16 * k + 16, :] = r
            out.append(carry[k] + r * r)
        return tuple(out)

    sums = lax.fori_loop(0, 128, second, zeros[:3], unroll=4)
    later = [total_of(sums[k]) for k in range(3)]
    beta = [later[k] / now[k] for k in range(3)]

    def third(d, carry):
        for k in range(3):
            at = slice(16 * k, 16 * k + 16)
            p_ref[d, at, :] = p_ref[d, at, :] + beta[k] * f_ref[d, at, :]
        return carry

    lax.fori_loop(0, 128, third, 0, unroll=4)
    rows = lax.broadcasted_iota(jnp.int32, (8, BS), 0)
    out = jnp.zeros((8, BS), jnp.float32)
    for k in range(3):
        out = jnp.where(rows == k, alpha[k], out)
        out = jnp.where(rows == 4 + k, later[k], out)
    coef_ref[...] = out


def cg_step(f, q):
    return pl.pallas_call(
        step_kernel,
        out_shape=[
            jax.ShapeDtypeStruct(f.shape, jnp.float32),
            jax.ShapeDtypeStruct((8, BS), jnp.float32),
        ],
        input_output_aliases={1: 0},
        compiler_params=pltpu.CompilerParams(vmem_limit_bytes=VMEM),
        cost_estimate=pl.CostEstimate(
            flops=f.size * 10, bytes_accessed=f.size * 12, transcendentals=0
        ),
    )(f, q)


def over_ctl(x):
    size = lax.axis_size("ctl")
    return lax.all_to_all(jnp.broadcast_to(x[None], (size,) + x.shape), "ctl", 0, 0, tiled=True)


def over_vol(x):
    return lax.all_gather(x, "vol", axis=0, tiled=True)


def place(block):
    return (((block >> 4) & 7) * 16 + (block >> 7)) * 48 + (block & 15)


def slot(block):
    return (((block >> 4) & 7) * 16 + (block >> 7)) * 16 + (block & 15)


def padded(rows):
    return jnp.pad(rows.transpose(1, 0, 2), ((0, 0), (0, 5), (0, 0)))


def body(sensitivity, sens_ids, ctl_coords, partners, node_coords, node_tiles):
    vol, ctl = lax.axis_index("vol"), lax.axis_index("ctl")
    device = vol * 16 + ctl
    own_coords = lax.dynamic_slice_in_dim(ctl_coords.reshape(3, 128, BS), vol * 16, 16, 1)
    ids = slot(sens_ids).astype(jnp.float32)
    lanes = jnp.arange(BS) // 16 == device % 8
    id_row = jnp.where(lanes, jnp.tile(ids, 8), 0.0)[None]
    payload = jnp.concatenate(
        [
            own_coords.reshape(48, BS),
            sensitivity.reshape(48, BS),
            jnp.pad(id_row, ((0, 7), (0, 0))),
        ],
        axis=0,
    )
    near = over_ctl(payload)
    coords = over_vol(near[:, :48])
    sens = over_vol(near[:, 48:])
    coords_rows = coords.reshape(128 * 48, BS)

    own = ctl * 128 + vol * 16 + jnp.arange(16, dtype=jnp.int32)
    mates = lax.dynamic_slice_in_dim(partners, vol * 16, 16, 0)
    lists = jnp.concatenate([own[:, None], mates], axis=1).reshape(-1)
    op_at = place(lists)
    node_at = place(node_tiles.reshape(-1))

    (op_tiles,) = make_tiles(op_at, padded(own_coords), coords_rows, None, 9, 2)
    want = jnp.broadcast_to(slot(lists).astype(jnp.float32)[:, None], (144, BS))
    f_near = spread(want, sens)
    sums = apply_tiles(
        jnp.arange(144, dtype=jnp.int32), op_tiles, f_near.reshape(3 * 144, BS), 9, 2, 144, 8.0
    )

    def back(total):
        return total[:, :3].transpose(1, 0, 2)

    f_own = f_near.reshape(3, 16, 9, BS)[:, :, 0]
    image = f_own + back(sums) * COUPLING
    near_image = over_ctl(image.reshape(48, BS))
    image_all = over_vol(near_image)
    f_all = spread_all(sens)
    node_rows = node_coords.reshape(3, 64, BS)
    node_tile, node_f = make_tiles(
        node_at, padded(node_rows), coords_rows, f_all.reshape(128 * 48, BS), 9, 4
    )
    p_all, coef = cg_step(f_all, image_all)
    p_rows = p_all.reshape(128 * 48, BS)
    sums = apply_tiles(op_at, op_tiles, p_rows, 9, 2, 16, 8.0)
    p_own = lax.dynamic_slice_in_dim(p_all, device, 1, 0).reshape(3, 16, BS)
    image = p_own + back(sums) * COUPLING
    dots = jnp.sum(p_own * image, axis=(1, 2))
    dot_row = jnp.broadcast_to(jnp.pad(dots, (0, BS - 3))[None], (128, BS))
    dots = jnp.sum(lax.all_to_all(dot_row, ("vol", "ctl"), 0, 0, tiled=True), axis=0)[:3]
    node_p = apply_tiles(node_at, node_tile, p_rows, 9, 4, 16, 1.0)

    alpha0 = coef[0:3, 0]
    alpha1 = coef[4:7, 0] / dots

    def mine(full):
        part = lax.dynamic_slice_in_dim(full.reshape(8, 16, 3, 16, BS), ctl, 1, 1)
        return part.reshape(8, 3, 16, BS).transpose(1, 0, 2, 3).reshape(3, 128, BS)

    weights = alpha0[:, None, None] * mine(f_all) + alpha1[:, None, None] * mine(p_all)
    shift = NODE_SCALE * (
        alpha0[:, None, None] * back(node_f) + alpha1[:, None, None] * back(node_p)
    )
    return weights.reshape(3, -1), shift.reshape(3, -1)


def solution(mesh):
    placed = (
        P(None, ("vol", "ctl")),
        P(("vol", "ctl")),
        P(None, "ctl"),
        P("ctl", None),
        P(None, ("vol", "ctl")),
        P(("vol", "ctl"), None),
    )
    return jax.shard_map(
        body,
        mesh=mesh,
        in_specs=placed,
        out_specs=(P(None, "ctl"), P(None, ("vol", "ctl"))),
        check_vma=False,
    )
```

```python
import functools

import jax
import jax.numpy as jnp
from jax import lax
from jax.experimental import pallas as pl
from jax.experimental.pallas import tpu as pltpu
from jax.sharding import PartitionSpec as P

BS = 128
COUPLING = 0.0625
NODE_SCALE = 0.25
VMEM = 56 * 1024 * 1024
CHUNK = 32
HEAD = 32


def whole(shape):
    return pl.BlockSpec(shape, lambda *a: (0,) * len(shape))


def lane_sums(group, acc_ref):
    ones = jnp.ones((BS, BS), jnp.bfloat16)
    eye = lax.broadcasted_iota(jnp.int32, (BS, BS), 0) == lax.broadcasted_iota(jnp.int32, (BS, BS), 1)
    out = []
    for k in range(3):
        part = acc_ref[k]
        high = part.astype(jnp.bfloat16)
        rest = (part - high.astype(jnp.float32)).astype(jnp.bfloat16)
        total = jnp.dot(high, ones, preferred_element_type=jnp.float32)
        total = total + jnp.dot(rest, ones, preferred_element_type=jnp.float32)
        out.append(
            [
                jnp.sum(jnp.where(eye, total[g * BS : (g + 1) * BS], 0.0), axis=0, keepdims=True)
                for g in range(group)
            ]
        )
    return out


def store_sums(group, acc_ref, sum_ref):
    rows = lax.broadcasted_iota(jnp.int32, (8, BS), 0)
    found = lane_sums(group, acc_ref)
    for g in range(group):
        out = jnp.zeros((8, BS), jnp.float32)
        for k in range(3):
            out = jnp.where(rows == k, found[k][g], out)
        sum_ref[g] = out


def tiles_kernel(reach, group, with_vec, idx_ref, pts_ref, ctl_ref, *refs):
    if with_vec:
        vec_ref, tile_ref, sum_ref, cols_ref, acc_ref = refs
    else:
        tile_ref, cols_ref = refs
    step = pl.program_id(0)
    for g in range(group):
        cols_ref[g] = jnp.transpose(pts_ref[g])

    def one(g, carry):
        base = (step * group + g) * reach
        for lo in range(0, BS, CHUNK):
            own = [jnp.broadcast_to(cols_ref[g, lo : lo + CHUNK, k : k + 1], (CHUNK, BS)) for k in range(3)]
            acc = [jnp.zeros((CHUNK, BS), jnp.float32) for _ in range(3)]
            for t in range(reach):
                at = idx_ref[base + t]
                dist = None
                for k in range(3):
                    gap = own[k] - ctl_ref[pl.ds(at + 16 * k, 1), :]
                    dist = gap * gap if dist is None else dist + gap * gap
                ratio = dist * lax.rsqrt(jnp.maximum(dist, 1e-30))
                inner = jnp.maximum(1.0 - ratio, 0.0)
                sq = inner * inner
                tile = (sq * sq) * (4.0 * ratio + 1.0)
                tile_ref[g * reach + t, lo : lo + CHUNK, :] = tile
                if with_vec:
                    for k in range(3):
                        acc[k] = acc[k] + tile * vec_ref[pl.ds(at + 16 * k, 1), :]
            if with_vec:
                for k in range(3):
                    acc_ref[k, pl.ds(pl.multiple_of(g * BS, BS) + lo, CHUNK), :] = acc[k]
        return carry

    lax.fori_loop(0, group, one, 0)
    if with_vec:
        store_sums(group, acc_ref, sum_ref)


def make_tiles(idx, pts, ctl, vec, reach, group):
    count = pts.shape[0]
    with_vec = vec is not None
    out_shape = [jax.ShapeDtypeStruct((count * reach, BS, BS), jnp.float32)]
    out_specs = [pl.BlockSpec((group * reach, BS, BS), lambda m, *_: (m, 0, 0))]
    scratch = [pltpu.VMEM((group, BS, 8), jnp.float32)]
    operands = [pts, ctl]
    in_specs = [pl.BlockSpec((group, 8, BS), lambda m, *_: (m, 0, 0)), whole(ctl.shape)]
    if with_vec:
        out_shape.append(jax.ShapeDtypeStruct((count, 8, BS), jnp.float32))
        out_specs.append(pl.BlockSpec((group, 8, BS), lambda m, *_: (m, 0, 0)))
        scratch.append(pltpu.VMEM((3, group * BS, BS), jnp.float32))
        operands.append(vec)
        in_specs.append(whole(vec.shape))
    elements = count * reach * BS * BS
    return pl.pallas_call(
        functools.partial(tiles_kernel, reach, group, with_vec),
        out_shape=out_shape,
        grid_spec=pltpu.PrefetchScalarGridSpec(
            num_scalar_prefetch=1,
            grid=(count // group,),
            in_specs=in_specs,
            out_specs=out_specs,
            scratch_shapes=scratch,
        ),
        compiler_params=pltpu.CompilerParams(vmem_limit_bytes=VMEM),
        cost_estimate=pl.CostEstimate(
            flops=elements * 24, bytes_accessed=elements * 4, transcendentals=elements
        ),
    )(idx, *operands)


def apply_kernel(reach, group, count, idx_ref, tile_ref, *refs):
    vec_refs, sum_refs, acc_refs = refs[:count], refs[count : 2 * count], refs[2 * count :]
    step = pl.program_id(0)

    def one(g, carry):
        base = (step * group + g) * reach
        start = pl.multiple_of(g * BS, BS)
        for lo in range(0, BS, CHUNK):
            acc = [[jnp.zeros((CHUNK, BS), jnp.float32) for _ in range(3)] for _ in vec_refs]
            for t in range(reach):
                at = idx_ref[base + t]
                tile = tile_ref[g * reach + t, lo : lo + CHUNK, :]
                for n, vec_ref in enumerate(vec_refs):
                    for k in range(3):
                        acc[n][k] = acc[n][k] + tile * vec_ref[pl.ds(at + 16 * k, 1), :]
            for n, acc_ref in enumerate(acc_refs):
                for k in range(3):
                    acc_ref[k, pl.ds(start + lo, CHUNK), :] = acc[n][k]
        return carry

    lax.fori_loop(0, group, one, 0)
    for acc_ref, sum_ref in zip(acc_refs, sum_refs):
        store_sums(group, acc_ref, sum_ref)


def apply_tiles(idx, tiles, vecs, reach, group):
    count = tiles.shape[0] // reach
    elements = tiles.size
    return pl.pallas_call(
        functools.partial(apply_kernel, reach, group, len(vecs)),
        out_shape=[jax.ShapeDtypeStruct((count, 8, BS), jnp.float32) for _ in vecs],
        grid_spec=pltpu.PrefetchScalarGridSpec(
            num_scalar_prefetch=1,
            grid=(count // group,),
            in_specs=[pl.BlockSpec((group * reach, BS, BS), lambda m, *_: (m, 0, 0))]
            + [whole(vec.shape) for vec in vecs],
            out_specs=[pl.BlockSpec((group, 8, BS), lambda m, *_: (m, 0, 0)) for _ in vecs],
            scratch_shapes=[pltpu.VMEM((3, group * BS, BS), jnp.float32) for _ in vecs],
        ),
        compiler_params=pltpu.CompilerParams(vmem_limit_bytes=VMEM),
        cost_estimate=pl.CostEstimate(
            flops=elements * 6 * len(vecs), bytes_accessed=elements * 4, transcendentals=0
        ),
    )(idx, tiles, *vecs)


def operator_sums(tile_ref, acc_ref, row):
    def one(g, carry):
        start = pl.multiple_of(g * BS, BS)
        for lo in range(0, BS, CHUNK):
            acc = [jnp.zeros((CHUNK, BS), jnp.float32) for _ in range(3)]
            for t in range(9):
                tile = tile_ref[g * 9 + t, lo : lo + CHUNK, :]
                for k in range(3):
                    part = row(g * 9 + t, k)
                    acc[k] = acc[k] + tile * (part * 8.0 if t == 0 else part)
            for k in range(3):
                acc_ref[k, pl.ds(start + lo, CHUNK), :] = acc[k]
        return carry

    lax.fori_loop(0, 16, one, 0)
    return lane_sums(16, acc_ref)


OPERATOR_SCRATCH = [
    pltpu.VMEM((144, BS, BS), jnp.float32),
    pltpu.VMEM((3, 16 * BS, BS), jnp.float32),
    pltpu.SemaphoreType.DMA,
]


def spread_kernel(want_ref, sens_ref, tile_hbm, own_ref, image_ref, near_ref, tile_ref, acc_ref, sem):
    copy = pltpu.make_async_copy(tile_hbm, tile_ref, sem)
    copy.start()
    ids = jnp.sum(sens_ref[:, 48, :].reshape(16, 8, BS), axis=1)
    want = want_ref[...]
    acc = [jnp.zeros((144, BS), jnp.float32) for _ in range(3)]
    for g in range(16):
        hot = (want == ids[g : g + 1, :]).astype(jnp.bfloat16)
        for k in range(3):
            part = sens_ref[8 * g : 8 * g + 8, 16 * k : 16 * k + 16, :].reshape(BS, BS)
            high = part.astype(jnp.bfloat16)
            rest = (part - high.astype(jnp.float32)).astype(jnp.bfloat16)
            acc[k] = acc[k] + jnp.dot(hot, high, preferred_element_type=jnp.float32)
            acc[k] = acc[k] + jnp.dot(hot, rest, preferred_element_type=jnp.float32)
    for k in range(3):
        near_ref[144 * k : 144 * k + 144] = acc[k]
    copy.wait()
    sums = operator_sums(tile_ref, acc_ref, lambda n, k: near_ref[pl.ds(n + 144 * k, 1), :])
    for k in range(3):
        for g in range(16):
            own = near_ref[144 * k + 9 * g : 144 * k + 9 * g + 1, :]
            own_ref[16 * k + g : 16 * k + g + 1, :] = own
            image_ref[16 * k + g : 16 * k + g + 1, :] = own + sums[k][g] * COUPLING


def spread_and_apply(want, sens, tiles):
    return pl.pallas_call(
        spread_kernel,
        out_shape=[jax.ShapeDtypeStruct((48, BS), jnp.float32)] * 2,
        in_specs=[
            pl.BlockSpec(memory_space=pltpu.VMEM),
            pl.BlockSpec(memory_space=pltpu.VMEM),
            pl.BlockSpec(memory_space=pl.ANY),
        ],
        scratch_shapes=[pltpu.VMEM((3 * 144, BS), jnp.float32)] + OPERATOR_SCRATCH,
        compiler_params=pltpu.CompilerParams(vmem_limit_bytes=VMEM),
        cost_estimate=pl.CostEstimate(
            flops=144 * 2048 * 384 * 4, bytes_accessed=tiles.size * 4, transcendentals=0
        ),
    )(want, sens, tiles)


def spread_all_kernel(sens_ref, out_ref, cut_ref, ids_ref):
    step = pl.program_id(0)

    @pl.when(step == 0)
    def _():
        ids_ref[...] = jnp.sum(sens_ref[:, 48, :].reshape(16, 8, BS), axis=1)
        for k in range(3):
            part = sens_ref[:, 16 * k : 16 * k + 16, :].reshape(2048, BS)
            high = part.astype(jnp.bfloat16)
            cut_ref[0, :, k * BS : (k + 1) * BS] = high
            cut_ref[1, :, k * BS : (k + 1) * BS] = (part - high.astype(jnp.float32)).astype(jnp.bfloat16)

    want = (lax.broadcasted_iota(jnp.int32, (256, BS), 0) + step * 256).astype(jnp.float32)
    hot = jnp.concatenate(
        [(want == ids_ref[g : g + 1, :]).astype(jnp.bfloat16) for g in range(16)], axis=1
    )
    acc = jnp.dot(hot, cut_ref[0], preferred_element_type=jnp.float32)
    acc = acc + jnp.dot(hot, cut_ref[1], preferred_element_type=jnp.float32)
    for k in range(3):
        out_ref[:, 16 * k : 16 * k + 16, :] = acc[:, k * BS : (k + 1) * BS].reshape(16, 16, BS)


def spread_all(sens):
    return pl.pallas_call(
        spread_all_kernel,
        out_shape=jax.ShapeDtypeStruct((128, 48, BS), jnp.float32),
        grid=(8,),
        in_specs=[whole(sens.shape)],
        out_specs=pl.BlockSpec((16, 48, BS), lambda m: (m, 0, 0)),
        scratch_shapes=[
            pltpu.VMEM((2, 2048, 3 * BS), jnp.bfloat16),
            pltpu.VMEM((16, BS), jnp.float32),
        ],
        compiler_params=pltpu.CompilerParams(vmem_limit_bytes=VMEM),
        cost_estimate=pl.CostEstimate(
            flops=2048 * 2048 * 384 * 4, bytes_accessed=sens.size * 8, transcendentals=0
        ),
    )(sens)


def total_of(part):
    return jnp.sum(jnp.sum(part, axis=0, keepdims=True), axis=1, keepdims=True)


def step_kernel(idx_ref, f_ref, q_ref, tile_hbm, p_ref, coef_ref, dot_ref, tile_ref, acc_ref, sem):
    copy = pltpu.make_async_copy(tile_hbm, tile_ref, sem)
    copy.start()
    zeros = tuple(jnp.zeros((16, BS), jnp.float32) for _ in range(6))

    def at(d, k):
        return pl.ds(pl.multiple_of(d * 48 + 16 * k, 16), 16)

    def first(d, carry):
        out = []
        for k in range(3):
            f, q = f_ref[at(d, k), :], q_ref[at(d, k), :]
            out += [carry[2 * k] + f * f, carry[2 * k + 1] + f * q]
        return tuple(out)

    sums = lax.fori_loop(0, 128, first, zeros, unroll=4)
    now = [total_of(sums[2 * k]) for k in range(3)]
    alpha = [now[k] / total_of(sums[2 * k + 1]) for k in range(3)]

    def second(d, carry):
        out = []
        for k in range(3):
            r = f_ref[at(d, k), :] - alpha[k] * q_ref[at(d, k), :]
            p_ref[at(d, k), :] = r
            out.append(carry[k] + r * r)
        return tuple(out)

    sums = lax.fori_loop(0, 128, second, zeros[:3], unroll=4)
    later = [total_of(sums[k]) for k in range(3)]
    beta = [later[k] / now[k] for k in range(3)]

    def third(d, carry):
        for k in range(3):
            p_ref[at(d, k), :] = p_ref[at(d, k), :] + beta[k] * f_ref[at(d, k), :]
        return carry

    lax.fori_loop(0, 128, third, 0, unroll=4)
    rows = lax.broadcasted_iota(jnp.int32, (8, BS), 0)
    out = jnp.zeros((8, BS), jnp.float32)
    for k in range(3):
        out = jnp.where(rows == k, alpha[k], out)
        out = jnp.where(rows == 4 + k, later[k], out)
    coef_ref[...] = out
    copy.wait()
    sums = operator_sums(tile_ref, acc_ref, lambda n, k: p_ref[pl.ds(idx_ref[n] + 16 * k, 1), :])
    lanes = lax.broadcasted_iota(jnp.int32, (1, BS), 1)
    out = jnp.zeros((1, BS), jnp.float32)
    for k in range(3):
        total = jnp.zeros((1, BS), jnp.float32)
        for g in range(16):
            own = p_ref[pl.ds(idx_ref[9 * g] + 16 * k, 1), :]
            total = total + own * (own + sums[k][g] * COUPLING)
        out = jnp.where(lanes == k, jnp.sum(total, axis=1, keepdims=True), out)
    dot_ref[...] = out


def step_and_apply(idx, f, q, tiles):
    vmem = pl.BlockSpec(memory_space=pltpu.VMEM)
    return pl.pallas_call(
        step_kernel,
        out_shape=[
            jax.ShapeDtypeStruct(f.shape, jnp.float32),
            jax.ShapeDtypeStruct((8, BS), jnp.float32),
            jax.ShapeDtypeStruct((1, BS), jnp.float32),
        ],
        in_specs=[pl.BlockSpec(memory_space=pltpu.SMEM), vmem, vmem, pl.BlockSpec(memory_space=pl.ANY)],
        scratch_shapes=OPERATOR_SCRATCH,
        input_output_aliases={2: 0},
        compiler_params=pltpu.CompilerParams(vmem_limit_bytes=VMEM),
        cost_estimate=pl.CostEstimate(
            flops=f.size * 10 + tiles.size * 6, bytes_accessed=tiles.size * 8, transcendentals=0
        ),
    )(idx, f, q, tiles)


def over_ctl(x):
    size = lax.axis_size("ctl")
    return lax.all_to_all(jnp.broadcast_to(x[None], (size,) + x.shape), "ctl", 0, 0, tiled=True)


def over_vol(x):
    return lax.all_gather(x, "vol", axis=0, tiled=True)


def place(block):
    return (((block >> 4) & 7) * 16 + (block >> 7)) * 48 + (block & 15)


def slot(block):
    return (((block >> 4) & 7) * 16 + (block >> 7)) * 16 + (block & 15)


def padded(rows):
    return jnp.pad(rows.transpose(1, 0, 2), ((0, 0), (0, 5), (0, 0)))


def body(sensitivity, sens_ids, ctl_coords, partners, node_coords, node_tiles):
    vol, ctl = lax.axis_index("vol"), lax.axis_index("ctl")
    device = vol * 16 + ctl
    own_coords = lax.dynamic_slice_in_dim(ctl_coords.reshape(3, 128, BS), vol * 16, 16, 1)
    ids = slot(sens_ids).astype(jnp.float32)
    lanes = jnp.arange(BS) // 16 == device % 8
    id_row = jnp.where(lanes, jnp.tile(ids, 8), 0.0)[None]
    payload = jnp.concatenate(
        [
            own_coords.reshape(48, BS),
            sensitivity.reshape(48, BS),
            jnp.pad(id_row, ((0, 7), (0, 0))),
        ],
        axis=0,
    )
    near = over_ctl(payload)
    coords = over_vol(near[:, :48])
    sens = over_vol(near[:, 48:])
    coords_rows = coords.reshape(128 * 48, BS)

    own = ctl * 128 + vol * 16 + jnp.arange(16, dtype=jnp.int32)
    mates = lax.dynamic_slice_in_dim(partners, vol * 16, 16, 0)
    lists = jnp.concatenate([own[:, None], mates], axis=1).reshape(-1)
    op_at = place(lists)
    node_at = place(node_tiles.reshape(-1))

    (op_tiles,) = make_tiles(op_at, padded(own_coords), coords_rows, None, 9, 4)
    points = padded(node_coords.reshape(3, 64, BS))
    head_at, tail_at = node_at[: HEAD * 9], node_at[HEAD * 9 :]
    (head_tiles,) = make_tiles(head_at, points[:HEAD], coords_rows, None, 9, 8)
    sens, head_tiles = lax.optimization_barrier((sens, head_tiles))
    want = jnp.broadcast_to(slot(lists).astype(jnp.float32)[:, None], (144, BS))
    f_own, image = spread_and_apply(want, sens, op_tiles)
    sens, image = lax.optimization_barrier((sens, image))
    near_image = over_ctl(image)
    f_all = spread_all(sens)
    image_all = over_vol(near_image).reshape(128 * 48, BS)
    f_rows = f_all.reshape(128 * 48, BS)
    tail_tiles, tail_f = make_tiles(tail_at, points[HEAD:], coords_rows, f_rows, 9, 8)
    image_all, tail_f = lax.optimization_barrier((image_all, tail_f))
    p_rows, coef, dot_row = step_and_apply(op_at, f_rows, image_all, op_tiles)
    dot_rows = lax.all_to_all(
        jnp.broadcast_to(dot_row, (128, BS)), ("vol", "ctl"), 0, 0, tiled=True
    )
    (tail_p,) = apply_tiles(tail_at, tail_tiles, [p_rows], 9, 8)
    head_f, head_p = apply_tiles(head_at, head_tiles, [f_rows, p_rows], 9, 8)
    dots = jnp.sum(dot_rows, axis=0)[:3]

    alpha0 = coef[0:3, 0]
    alpha1 = coef[4:7, 0] / dots

    def mine(full):
        part = lax.dynamic_slice_in_dim(full.reshape(8, 16, 3, 16, BS), ctl, 1, 1)
        return part.reshape(8, 3, 16, BS).transpose(1, 0, 2, 3).reshape(3, 128, BS)

    def back(head, tail):
        return jnp.concatenate([head[:, :3], tail[:, :3]], axis=0).transpose(1, 0, 2)

    weights = alpha0[:, None, None] * mine(f_rows) + alpha1[:, None, None] * mine(p_rows)
    shift = NODE_SCALE * (
        alpha0[:, None, None] * back(head_f, tail_f) + alpha1[:, None, None] * back(head_p, tail_p)
    )
    return weights.reshape(3, -1), shift.reshape(3, -1)


def solution(mesh):
    placed = (
        P(None, ("vol", "ctl")),
        P(("vol", "ctl")),
        P(None, "ctl"),
        P("ctl", None),
        P(None, ("vol", "ctl")),
        P(("vol", "ctl"), None),
    )
    return jax.shard_map(
        body,
        mesh=mesh,
        in_specs=placed,
        out_specs=(P(None, "ctl"), P(None, ("vol", "ctl"))),
        check_vma=False,
    )
```

```python
import functools

import jax
import jax.numpy as jnp
from jax import lax
from jax.experimental import pallas as pl
from jax.experimental.pallas import tpu as pltpu
from jax.sharding import PartitionSpec as P

BS = 128
COUPLING = 0.0625
NODE_SCALE = 0.25
VMEM = 56 * 1024 * 1024
CHUNK = 32
HEAD = 32


def whole(shape):
    return pl.BlockSpec(shape, lambda *a: (0,) * len(shape))


def lane_sums(group, acc_ref):
    ones = jnp.ones((BS, BS), jnp.bfloat16)
    eye = lax.broadcasted_iota(jnp.int32, (BS, BS), 0) == lax.broadcasted_iota(jnp.int32, (BS, BS), 1)
    out = []
    for k in range(3):
        part = acc_ref[k]
        high = part.astype(jnp.bfloat16)
        rest = (part - high.astype(jnp.float32)).astype(jnp.bfloat16)
        total = jnp.dot(high, ones, preferred_element_type=jnp.float32)
        total = total + jnp.dot(rest, ones, preferred_element_type=jnp.float32)
        out.append(
            [
                jnp.sum(jnp.where(eye, total[g * BS : (g + 1) * BS], 0.0), axis=0, keepdims=True)
                for g in range(group)
            ]
        )
    return out


def store_sums(group, acc_ref, sum_ref):
    rows = lax.broadcasted_iota(jnp.int32, (8, BS), 0)
    found = lane_sums(group, acc_ref)
    for g in range(group):
        out = jnp.zeros((8, BS), jnp.float32)
        for k in range(3):
            out = jnp.where(rows == k, found[k][g], out)
        sum_ref[g] = out


def tiles_kernel(reach, group, idx_ref, pts_ref, ctl_ref, *refs):
    tile_ref, cols_ref = refs[-2:]
    step = pl.program_id(0)
    for g in range(group):
        cols_ref[g] = jnp.transpose(pts_ref[g])

    def one(g, carry):
        base = (step * group + g) * reach
        for lo in range(0, BS, CHUNK):
            own = [
                jnp.broadcast_to(cols_ref[g, lo : lo + CHUNK, k : k + 1], (CHUNK, BS))
                for k in range(3)
            ]
            for t in range(reach):
                at = idx_ref[base + t]
                dist = None
                for k in range(3):
                    gap = own[k] - ctl_ref[pl.ds(at + 16 * k, 1), :]
                    dist = gap * gap if dist is None else dist + gap * gap
                ratio = dist * lax.rsqrt(jnp.maximum(dist, 1e-30))
                inner = jnp.maximum(1.0 - ratio, 0.0)
                sq = inner * inner
                tile = (sq * sq) * (4.0 * ratio + 1.0)
                tile_ref[g * reach + t, lo : lo + CHUNK, :] = tile
        return carry

    lax.fori_loop(0, group, one, 0)


def make_tiles(idx, pts, ctl, reach, group, count=None, skip=0, into=None):
    here = pts.shape[0]
    count = count or here
    first = skip // group
    operands = [pts, ctl]
    in_specs = [pl.BlockSpec((group, 8, BS), lambda m, *_: (m, 0, 0)), whole(ctl.shape)]
    alias = {}
    if into is not None:
        operands.append(into)
        in_specs.append(pl.BlockSpec(memory_space=pl.ANY))
        alias = {3: 0}
    elements = here * reach * BS * BS
    return pl.pallas_call(
        functools.partial(tiles_kernel, reach, group),
        out_shape=jax.ShapeDtypeStruct((count * reach, BS, BS), jnp.float32),
        grid_spec=pltpu.PrefetchScalarGridSpec(
            num_scalar_prefetch=1,
            grid=(here // group,),
            in_specs=in_specs,
            out_specs=pl.BlockSpec((group * reach, BS, BS), lambda m, *_: (m + first, 0, 0)),
            scratch_shapes=[pltpu.VMEM((group, BS, 8), jnp.float32)],
        ),
        input_output_aliases=alias,
        compiler_params=pltpu.CompilerParams(vmem_limit_bytes=VMEM),
        cost_estimate=pl.CostEstimate(
            flops=elements * 24, bytes_accessed=elements * 4, transcendentals=elements
        ),
    )(idx, *operands)


def apply_kernel(reach, group, count, idx_ref, tile_ref, *refs):
    vec_refs, sum_refs, acc_refs = refs[:count], refs[count : 2 * count], refs[2 * count :]
    step = pl.program_id(0)

    def one(g, carry):
        base = (step * group + g) * reach
        start = pl.multiple_of(g * BS, BS)
        for lo in range(0, BS, CHUNK):
            acc = [[jnp.zeros((CHUNK, BS), jnp.float32) for _ in range(3)] for _ in vec_refs]
            for t in range(reach):
                at = idx_ref[base + t]
                tile = tile_ref[g * reach + t, lo : lo + CHUNK, :]
                for n, vec_ref in enumerate(vec_refs):
                    for k in range(3):
                        acc[n][k] = acc[n][k] + tile * vec_ref[pl.ds(at + 16 * k, 1), :]
            for n, acc_ref in enumerate(acc_refs):
                for k in range(3):
                    acc_ref[k, pl.ds(start + lo, CHUNK), :] = acc[n][k]
        return carry

    lax.fori_loop(0, group, one, 0)
    for acc_ref, sum_ref in zip(acc_refs, sum_refs):
        store_sums(group, acc_ref, sum_ref)


def apply_tiles(idx, tiles, vecs, reach, group):
    count = tiles.shape[0] // reach
    elements = tiles.size
    return pl.pallas_call(
        functools.partial(apply_kernel, reach, group, len(vecs)),
        out_shape=[jax.ShapeDtypeStruct((count, 8, BS), jnp.float32) for _ in vecs],
        grid_spec=pltpu.PrefetchScalarGridSpec(
            num_scalar_prefetch=1,
            grid=(count // group,),
            in_specs=[pl.BlockSpec((group * reach, BS, BS), lambda m, *_: (m, 0, 0))]
            + [whole(vec.shape) for vec in vecs],
            out_specs=[pl.BlockSpec((group, 8, BS), lambda m, *_: (m, 0, 0)) for _ in vecs],
            scratch_shapes=[pltpu.VMEM((3, group * BS, BS), jnp.float32) for _ in vecs],
        ),
        compiler_params=pltpu.CompilerParams(vmem_limit_bytes=VMEM),
        cost_estimate=pl.CostEstimate(
            flops=elements * 6 * len(vecs), bytes_accessed=elements * 4, transcendentals=0
        ),
    )(idx, tiles, *vecs)


def operator_sums(tile_ref, acc_ref, row):
    def one(g, carry):
        start = pl.multiple_of(g * BS, BS)
        for lo in range(0, BS, CHUNK):
            acc = [jnp.zeros((CHUNK, BS), jnp.float32) for _ in range(3)]
            for t in range(9):
                tile = tile_ref[g * 9 + t, lo : lo + CHUNK, :]
                for k in range(3):
                    part = row(g * 9 + t, k)
                    acc[k] = acc[k] + tile * (part * 8.0 if t == 0 else part)
            for k in range(3):
                acc_ref[k, pl.ds(start + lo, CHUNK), :] = acc[k]
        return carry

    lax.fori_loop(0, 16, one, 0)
    return lane_sums(16, acc_ref)


OPERATOR_SCRATCH = [
    pltpu.VMEM((144, BS, BS), jnp.float32),
    pltpu.VMEM((3, 16 * BS, BS), jnp.float32),
    pltpu.SemaphoreType.DMA,
]


def spread_kernel(want_ref, sens_ref, tile_hbm, own_ref, image_ref, near_ref, tile_ref, acc_ref, sem):
    copy = pltpu.make_async_copy(tile_hbm, tile_ref, sem)
    copy.start()
    ids = jnp.sum(sens_ref[:, 48, :].reshape(16, 8, BS), axis=1)
    want = want_ref[...]
    acc = [jnp.zeros((144, BS), jnp.float32) for _ in range(3)]
    for g in range(16):
        hot = (want == ids[g : g + 1, :]).astype(jnp.bfloat16)
        for k in range(3):
            part = sens_ref[8 * g : 8 * g + 8, 16 * k : 16 * k + 16, :].reshape(BS, BS)
            high = part.astype(jnp.bfloat16)
            rest = (part - high.astype(jnp.float32)).astype(jnp.bfloat16)
            acc[k] = acc[k] + jnp.dot(hot, high, preferred_element_type=jnp.float32)
            acc[k] = acc[k] + jnp.dot(hot, rest, preferred_element_type=jnp.float32)
    for k in range(3):
        near_ref[144 * k : 144 * k + 144] = acc[k]
    copy.wait()
    sums = operator_sums(tile_ref, acc_ref, lambda n, k: near_ref[pl.ds(n + 144 * k, 1), :])
    for k in range(3):
        for g in range(16):
            own = near_ref[144 * k + 9 * g : 144 * k + 9 * g + 1, :]
            own_ref[16 * k + g : 16 * k + g + 1, :] = own
            image_ref[16 * k + g : 16 * k + g + 1, :] = own + sums[k][g] * COUPLING


def spread_and_apply(want, sens, tiles):
    return pl.pallas_call(
        spread_kernel,
        out_shape=[jax.ShapeDtypeStruct((48, BS), jnp.float32)] * 2,
        in_specs=[
            pl.BlockSpec(memory_space=pltpu.VMEM),
            pl.BlockSpec(memory_space=pltpu.VMEM),
            pl.BlockSpec(memory_space=pl.ANY),
        ],
        scratch_shapes=[pltpu.VMEM((3 * 144, BS), jnp.float32)] + OPERATOR_SCRATCH,
        compiler_params=pltpu.CompilerParams(vmem_limit_bytes=VMEM),
        cost_estimate=pl.CostEstimate(
            flops=144 * 2048 * 384 * 4, bytes_accessed=tiles.size * 4, transcendentals=0
        ),
    )(want, sens, tiles)


def spread_all_kernel(sens_ref, out_ref, cut_ref, ids_ref):
    step = pl.program_id(0)

    @pl.when(step == 0)
    def _():
        ids_ref[...] = jnp.sum(sens_ref[:, 48, :].reshape(16, 8, BS), axis=1)
        for k in range(3):
            part = sens_ref[:, 16 * k : 16 * k + 16, :].reshape(2048, BS)
            high = part.astype(jnp.bfloat16)
            cut_ref[0, :, k * BS : (k + 1) * BS] = high
            cut_ref[1, :, k * BS : (k + 1) * BS] = (part - high.astype(jnp.float32)).astype(jnp.bfloat16)

    want = (lax.broadcasted_iota(jnp.int32, (256, BS), 0) + step * 256).astype(jnp.float32)
    hot = jnp.concatenate(
        [(want == ids_ref[g : g + 1, :]).astype(jnp.bfloat16) for g in range(16)], axis=1
    )
    acc = jnp.dot(hot, cut_ref[0], preferred_element_type=jnp.float32)
    acc = acc + jnp.dot(hot, cut_ref[1], preferred_element_type=jnp.float32)
    for k in range(3):
        out_ref[:, 16 * k : 16 * k + 16, :] = acc[:, k * BS : (k + 1) * BS].reshape(16, 16, BS)


def spread_all(sens):
    return pl.pallas_call(
        spread_all_kernel,
        out_shape=jax.ShapeDtypeStruct((128, 48, BS), jnp.float32),
        grid=(8,),
        in_specs=[whole(sens.shape)],
        out_specs=pl.BlockSpec((16, 48, BS), lambda m: (m, 0, 0)),
        scratch_shapes=[
            pltpu.VMEM((2, 2048, 3 * BS), jnp.bfloat16),
            pltpu.VMEM((16, BS), jnp.float32),
        ],
        compiler_params=pltpu.CompilerParams(vmem_limit_bytes=VMEM),
        cost_estimate=pl.CostEstimate(
            flops=2048 * 2048 * 384 * 4, bytes_accessed=sens.size * 8, transcendentals=0
        ),
    )(sens)


def total_of(part):
    return jnp.sum(jnp.sum(part, axis=0, keepdims=True), axis=1, keepdims=True)


def step_kernel(idx_ref, f_ref, q_ref, tile_hbm, p_ref, coef_ref, dot_ref, tile_ref, acc_ref, sem):
    copy = pltpu.make_async_copy(tile_hbm, tile_ref, sem)
    copy.start()
    zeros = tuple(jnp.zeros((16, BS), jnp.float32) for _ in range(6))

    def at(d, k):
        return pl.ds(pl.multiple_of(d * 48 + 16 * k, 16), 16)

    def first(d, carry):
        out = []
        for k in range(3):
            f, q = f_ref[at(d, k), :], q_ref[at(d, k), :]
            out += [carry[2 * k] + f * f, carry[2 * k + 1] + f * q]
        return tuple(out)

    sums = lax.fori_loop(0, 128, first, zeros, unroll=4)
    now = [total_of(sums[2 * k]) for k in range(3)]
    alpha = [now[k] / total_of(sums[2 * k + 1]) for k in range(3)]

    def second(d, carry):
        out = []
        for k in range(3):
            r = f_ref[at(d, k), :] - alpha[k] * q_ref[at(d, k), :]
            p_ref[at(d, k), :] = r
            out.append(carry[k] + r * r)
        return tuple(out)

    sums = lax.fori_loop(0, 128, second, zeros[:3], unroll=4)
    later = [total_of(sums[k]) for k in range(3)]
    beta = [later[k] / now[k] for k in range(3)]

    def third(d, carry):
        for k in range(3):
            p_ref[at(d, k), :] = p_ref[at(d, k), :] + beta[k] * f_ref[at(d, k), :]
        return carry

    lax.fori_loop(0, 128, third, 0, unroll=4)
    rows = lax.broadcasted_iota(jnp.int32, (8, BS), 0)
    out = jnp.zeros((8, BS), jnp.float32)
    for k in range(3):
        out = jnp.where(rows == k, alpha[k], out)
        out = jnp.where(rows == 4 + k, later[k], out)
    coef_ref[...] = out
    copy.wait()
    sums = operator_sums(tile_ref, acc_ref, lambda n, k: p_ref[pl.ds(idx_ref[n] + 16 * k, 1), :])
    lanes = lax.broadcasted_iota(jnp.int32, (1, BS), 1)
    out = jnp.zeros((1, BS), jnp.float32)
    for k in range(3):
        total = jnp.zeros((1, BS), jnp.float32)
        for g in range(16):
            own = p_ref[pl.ds(idx_ref[9 * g] + 16 * k, 1), :]
            total = total + own * (own + sums[k][g] * COUPLING)
        out = jnp.where(lanes == k, jnp.sum(total, axis=1, keepdims=True), out)
    dot_ref[...] = out


def step_and_apply(idx, f, q, tiles):
    vmem = pl.BlockSpec(memory_space=pltpu.VMEM)
    return pl.pallas_call(
        step_kernel,
        out_shape=[
            jax.ShapeDtypeStruct(f.shape, jnp.float32),
            jax.ShapeDtypeStruct((8, BS), jnp.float32),
            jax.ShapeDtypeStruct((1, BS), jnp.float32),
        ],
        in_specs=[pl.BlockSpec(memory_space=pltpu.SMEM), vmem, vmem, pl.BlockSpec(memory_space=pl.ANY)],
        scratch_shapes=OPERATOR_SCRATCH,
        input_output_aliases={2: 0},
        compiler_params=pltpu.CompilerParams(vmem_limit_bytes=VMEM),
        cost_estimate=pl.CostEstimate(
            flops=f.size * 10 + tiles.size * 6, bytes_accessed=tiles.size * 8, transcendentals=0
        ),
    )(idx, f, q, tiles)


def copies(x):
    return jnp.broadcast_to(x[None], (lax.axis_size("ctl"),) + x.shape)


def over_ctl(x):
    return lax.all_to_all(x, "ctl", 0, 0, tiled=True)


def over_vol(x):
    return lax.all_gather(x, "vol", axis=0, tiled=True)


def place(block):
    return (((block >> 4) & 7) * 16 + (block >> 7)) * 48 + (block & 15)


def slot(block):
    return (((block >> 4) & 7) * 16 + (block >> 7)) * 16 + (block & 15)


def padded(rows):
    return jnp.pad(rows.transpose(1, 0, 2), ((0, 0), (0, 5), (0, 0)))


def body(sensitivity, sens_ids, ctl_coords, partners, node_coords, node_tiles):
    vol, ctl = lax.axis_index("vol"), lax.axis_index("ctl")
    device = vol * 16 + ctl
    own_coords = lax.dynamic_slice_in_dim(ctl_coords.reshape(3, 128, BS), vol * 16, 16, 1)
    ids = slot(sens_ids).astype(jnp.float32)
    lanes = jnp.arange(BS) // 16 == device % 8
    id_row = jnp.where(lanes, jnp.tile(ids, 8), 0.0)[None]
    payload = jnp.concatenate(
        [
            own_coords.reshape(48, BS),
            sensitivity.reshape(48, BS),
            jnp.pad(id_row, ((0, 7), (0, 0))),
        ],
        axis=0,
    )
    near = over_ctl(copies(payload))
    coords = over_vol(near[:, :48])
    sens = over_vol(near[:, 48:])
    coords_rows = coords.reshape(128 * 48, BS)

    own = ctl * 128 + vol * 16 + jnp.arange(16, dtype=jnp.int32)
    mates = lax.dynamic_slice_in_dim(partners, vol * 16, 16, 0)
    lists = jnp.concatenate([own[:, None], mates], axis=1).reshape(-1)
    op_at = place(lists)
    node_at = place(node_tiles.reshape(-1))

    op_tiles = make_tiles(op_at, padded(own_coords), coords_rows, 9, 4)
    points = padded(node_coords.reshape(3, 64, BS))
    head_at, tail_at = node_at[: HEAD * 9], node_at[HEAD * 9 :]
    tiles = make_tiles(head_at, points[:HEAD], coords_rows, 9, 8, count=64)
    sens, tiles = lax.optimization_barrier((sens, tiles))
    want = jnp.broadcast_to(slot(lists).astype(jnp.float32)[:, None], (144, BS))
    f_own, image = spread_and_apply(want, sens, op_tiles)
    image, sens = lax.optimization_barrier((copies(image), sens))
    near_image = over_ctl(image)
    f_all = spread_all(sens)
    near_image, f_all = lax.optimization_barrier((near_image, f_all))
    image_all = over_vol(near_image).reshape(128 * 48, BS)
    f_rows = f_all.reshape(128 * 48, BS)
    tiles = make_tiles(tail_at, points[HEAD:], coords_rows, 9, 8, 64, HEAD, tiles)
    image_all, tiles = lax.optimization_barrier((image_all, tiles))
    p_rows, coef, dot_row = step_and_apply(op_at, f_rows, image_all, op_tiles)

    def mine(full):
        part = lax.dynamic_slice_in_dim(full.reshape(8, 16, 3, 16, BS), ctl, 1, 1)
        return part.reshape(8, 3, 16, BS).transpose(1, 0, 2, 3).reshape(3, 128, BS)

    f_mine, p_mine = mine(f_rows), mine(p_rows)
    alpha0 = coef[0:3, 0]
    dot_rows, p_rows, f_mine, p_mine = lax.optimization_barrier(
        (jnp.broadcast_to(dot_row[None], (128, 8, BS)), p_rows, f_mine, p_mine)
    )
    dot_rows = lax.all_to_all(dot_rows, ("vol", "ctl"), 0, 0, tiled=True)
    node_f, node_p = apply_tiles(node_at, tiles, [f_rows, p_rows], 9, 8)
    dot_rows, node_f, node_p = lax.optimization_barrier((dot_rows, node_f, node_p))
    alpha1 = coef[4:7, 0] / jnp.sum(dot_rows[:, 0], axis=0)[:3]

    def back(sums):
        return sums[:, :3].transpose(1, 0, 2)

    weights = alpha0[:, None, None] * f_mine + alpha1[:, None, None] * p_mine
    shift = NODE_SCALE * (
        alpha0[:, None, None] * back(node_f) + alpha1[:, None, None] * back(node_p)
    )
    return weights.reshape(3, -1), shift.reshape(3, -1)


def solution(mesh):
    placed = (
        P(None, ("vol", "ctl")),
        P(("vol", "ctl")),
        P(None, "ctl"),
        P("ctl", None),
        P(None, ("vol", "ctl")),
        P(("vol", "ctl"), None),
    )
    return jax.shard_map(
        body,
        mesh=mesh,
        in_specs=placed,
        out_specs=(P(None, "ctl"), P(None, ("vol", "ctl"))),
        check_vma=False,
    )
```

```python
import functools

import jax
import jax.numpy as jnp
from jax import lax
from jax.experimental import pallas as pl
from jax.experimental.pallas import tpu as pltpu
from jax.sharding import PartitionSpec as P

BS = 128
COUPLING = 0.0625
NODE_SCALE = 0.25
VMEM = 56 * 1024 * 1024
CHUNK = 32


def whole(shape):
    return pl.BlockSpec(shape, lambda *a: (0,) * len(shape))


def lane_sums(group, acc_ref):
    ones = jnp.ones((BS, BS), jnp.bfloat16)
    eye = lax.broadcasted_iota(jnp.int32, (BS, BS), 0) == lax.broadcasted_iota(jnp.int32, (BS, BS), 1)
    out = []
    for k in range(3):
        part = acc_ref[k]
        high = part.astype(jnp.bfloat16)
        rest = (part - high.astype(jnp.float32)).astype(jnp.bfloat16)
        total = jnp.dot(high, ones, preferred_element_type=jnp.float32)
        total = total + jnp.dot(rest, ones, preferred_element_type=jnp.float32)
        out.append(
            [
                jnp.sum(jnp.where(eye, total[g * BS : (g + 1) * BS], 0.0), axis=0, keepdims=True)
                for g in range(group)
            ]
        )
    return out


def store_sums(group, acc_ref, sum_ref):
    rows = lax.broadcasted_iota(jnp.int32, (8, BS), 0)
    found = lane_sums(group, acc_ref)
    for g in range(group):
        out = jnp.zeros((8, BS), jnp.float32)
        for k in range(3):
            out = jnp.where(rows == k, found[k][g], out)
        sum_ref[g] = out


def tiles_kernel(reach, group, idx_ref, pts_ref, ctl_ref, tile_ref, cols_ref):
    step = pl.program_id(0)
    for g in range(group):
        cols_ref[g] = jnp.transpose(pts_ref[g])

    def one(g, carry):
        base = (step * group + g) * reach
        for lo in range(0, BS, CHUNK):
            own = [
                jnp.broadcast_to(cols_ref[g, lo : lo + CHUNK, k : k + 1], (CHUNK, BS))
                for k in range(3)
            ]
            for t in range(reach):
                at = idx_ref[base + t]
                dist = None
                for k in range(3):
                    gap = own[k] - ctl_ref[pl.ds(at + 64 * k, 1), :]
                    dist = gap * gap if dist is None else dist + gap * gap
                ratio = dist * lax.rsqrt(jnp.maximum(dist, 1e-30))
                inner = jnp.maximum(1.0 - ratio, 0.0)
                sq = inner * inner
                tile = (sq * sq) * (4.0 * ratio + 1.0)
                tile_ref[g * reach + t, lo : lo + CHUNK, :] = tile
        return carry

    lax.fori_loop(0, group, one, 0)


def make_tiles(idx, pts, ctl, reach, group):
    count = pts.shape[0]
    in_specs = [pl.BlockSpec((group, 8, BS), lambda m, *_: (m, 0, 0)), whole(ctl.shape)]
    elements = count * reach * BS * BS
    return pl.pallas_call(
        functools.partial(tiles_kernel, reach, group),
        out_shape=jax.ShapeDtypeStruct((count * reach, BS, BS), jnp.float32),
        grid_spec=pltpu.PrefetchScalarGridSpec(
            num_scalar_prefetch=1,
            grid=(count // group,),
            in_specs=in_specs,
            out_specs=pl.BlockSpec((group * reach, BS, BS), lambda m, *_: (m, 0, 0)),
            scratch_shapes=[pltpu.VMEM((group, BS, 8), jnp.float32)],
        ),
        compiler_params=pltpu.CompilerParams(vmem_limit_bytes=VMEM),
        cost_estimate=pl.CostEstimate(
            flops=elements * 24, bytes_accessed=elements * 4, transcendentals=elements
        ),
    )(idx, pts, ctl)


def apply_kernel(reach, group, count, idx_ref, tile_ref, *refs):
    vec_refs, sum_refs, acc_refs = refs[:count], refs[count : 2 * count], refs[2 * count :]
    step = pl.program_id(0)

    def one(g, carry):
        base = (step * group + g) * reach
        start = pl.multiple_of(g * BS, BS)
        for lo in range(0, BS, CHUNK):
            acc = [[jnp.zeros((CHUNK, BS), jnp.float32) for _ in range(3)] for _ in vec_refs]
            for t in range(reach):
                at = idx_ref[base + t]
                tile = tile_ref[g * reach + t, lo : lo + CHUNK, :]
                for n, vec_ref in enumerate(vec_refs):
                    for k in range(3):
                        acc[n][k] = acc[n][k] + tile * vec_ref[pl.ds(at + 16 * k, 1), :]
            for n, acc_ref in enumerate(acc_refs):
                for k in range(3):
                    acc_ref[k, pl.ds(start + lo, CHUNK), :] = acc[n][k]
        return carry

    lax.fori_loop(0, group, one, 0)
    for acc_ref, sum_ref in zip(acc_refs, sum_refs):
        store_sums(group, acc_ref, sum_ref)


def apply_tiles(idx, tiles, vecs, reach, group):
    count = tiles.shape[0] // reach
    elements = tiles.size
    return pl.pallas_call(
        functools.partial(apply_kernel, reach, group, len(vecs)),
        out_shape=[jax.ShapeDtypeStruct((count, 8, BS), jnp.float32) for _ in vecs],
        grid_spec=pltpu.PrefetchScalarGridSpec(
            num_scalar_prefetch=1,
            grid=(count // group,),
            in_specs=[pl.BlockSpec((group * reach, BS, BS), lambda m, *_: (m, 0, 0))]
            + [whole(vec.shape) for vec in vecs],
            out_specs=[pl.BlockSpec((group, 8, BS), lambda m, *_: (m, 0, 0)) for _ in vecs],
            scratch_shapes=[pltpu.VMEM((3, group * BS, BS), jnp.float32) for _ in vecs],
        ),
        compiler_params=pltpu.CompilerParams(vmem_limit_bytes=VMEM),
        cost_estimate=pl.CostEstimate(
            flops=elements * 6 * len(vecs), bytes_accessed=elements * 4, transcendentals=0
        ),
    )(idx, tiles, *vecs)


def operator_sums(tile_ref, acc_ref, row):
    def one(g, carry):
        start = pl.multiple_of(g * BS, BS)
        for lo in range(0, BS, CHUNK):
            acc = [jnp.zeros((CHUNK, BS), jnp.float32) for _ in range(3)]
            for t in range(9):
                tile = tile_ref[g * 9 + t, lo : lo + CHUNK, :]
                for k in range(3):
                    part = row(g * 9 + t, k)
                    acc[k] = acc[k] + tile * (part * 8.0 if t == 0 else part)
            for k in range(3):
                acc_ref[k, pl.ds(start + lo, CHUNK), :] = acc[k]
        return carry

    lax.fori_loop(0, 16, one, 0)
    return lane_sums(16, acc_ref)


OPERATOR_SCRATCH = [
    pltpu.VMEM((144, BS, BS), jnp.float32),
    pltpu.VMEM((3, 16 * BS, BS), jnp.float32),
    pltpu.SemaphoreType.DMA,
]


def spread_kernel(want_ref, sens_ref, tile_hbm, own_ref, image_ref, near_ref, tile_ref, acc_ref, sem):
    copy = pltpu.make_async_copy(tile_hbm, tile_ref, sem)
    copy.start()
    ids = jnp.sum(sens_ref[:, 48, :].reshape(16, 8, BS), axis=1)
    want = want_ref[...]
    acc = [jnp.zeros((144, BS), jnp.float32) for _ in range(3)]
    for g in range(16):
        hot = (want == ids[g : g + 1, :]).astype(jnp.bfloat16)
        for k in range(3):
            part = sens_ref[8 * g : 8 * g + 8, 16 * k : 16 * k + 16, :].reshape(BS, BS)
            high = part.astype(jnp.bfloat16)
            rest = (part - high.astype(jnp.float32)).astype(jnp.bfloat16)
            acc[k] = acc[k] + jnp.dot(hot, high, preferred_element_type=jnp.float32)
            acc[k] = acc[k] + jnp.dot(hot, rest, preferred_element_type=jnp.float32)
    for k in range(3):
        near_ref[144 * k : 144 * k + 144] = acc[k]
    copy.wait()
    sums = operator_sums(tile_ref, acc_ref, lambda n, k: near_ref[pl.ds(n + 144 * k, 1), :])
    for k in range(3):
        for g in range(16):
            own = near_ref[144 * k + 9 * g : 144 * k + 9 * g + 1, :]
            own_ref[16 * k + g : 16 * k + g + 1, :] = own
            image_ref[16 * k + g : 16 * k + g + 1, :] = own + sums[k][g] * COUPLING


def spread_and_apply(want, sens, tiles):
    return pl.pallas_call(
        spread_kernel,
        out_shape=[jax.ShapeDtypeStruct((48, BS), jnp.float32)] * 2,
        in_specs=[
            pl.BlockSpec(memory_space=pltpu.VMEM),
            pl.BlockSpec(memory_space=pltpu.VMEM),
            pl.BlockSpec(memory_space=pl.ANY),
        ],
        scratch_shapes=[pltpu.VMEM((3 * 144, BS), jnp.float32)] + OPERATOR_SCRATCH,
        compiler_params=pltpu.CompilerParams(vmem_limit_bytes=VMEM),
        cost_estimate=pl.CostEstimate(
            flops=144 * 2048 * 384 * 4, bytes_accessed=tiles.size * 4, transcendentals=0
        ),
    )(want, sens, tiles)


def spread_all_kernel(sens_ref, out_ref, cut_ref, ids_ref):
    step = pl.program_id(0)

    @pl.when(step == 0)
    def _():
        ids_ref[...] = jnp.sum(sens_ref[:, 48, :].reshape(16, 8, BS), axis=1)
        for k in range(3):
            part = sens_ref[:, 16 * k : 16 * k + 16, :].reshape(2048, BS)
            high = part.astype(jnp.bfloat16)
            cut_ref[0, :, k * BS : (k + 1) * BS] = high
            cut_ref[1, :, k * BS : (k + 1) * BS] = (part - high.astype(jnp.float32)).astype(jnp.bfloat16)

    want = (lax.broadcasted_iota(jnp.int32, (256, BS), 0) + step * 256).astype(jnp.float32)
    hot = jnp.concatenate(
        [(want == ids_ref[g : g + 1, :]).astype(jnp.bfloat16) for g in range(16)], axis=1
    )
    acc = jnp.dot(hot, cut_ref[0], preferred_element_type=jnp.float32)
    acc = acc + jnp.dot(hot, cut_ref[1], preferred_element_type=jnp.float32)
    for k in range(3):
        out_ref[:, 16 * k : 16 * k + 16, :] = acc[:, k * BS : (k + 1) * BS].reshape(16, 16, BS)


def spread_all(sens):
    return pl.pallas_call(
        spread_all_kernel,
        out_shape=jax.ShapeDtypeStruct((128, 48, BS), jnp.float32),
        grid=(8,),
        in_specs=[whole(sens.shape)],
        out_specs=pl.BlockSpec((16, 48, BS), lambda m: (m, 0, 0)),
        scratch_shapes=[
            pltpu.VMEM((2, 2048, 3 * BS), jnp.bfloat16),
            pltpu.VMEM((16, BS), jnp.float32),
        ],
        compiler_params=pltpu.CompilerParams(vmem_limit_bytes=VMEM),
        cost_estimate=pl.CostEstimate(
            flops=2048 * 2048 * 384 * 4, bytes_accessed=sens.size * 8, transcendentals=0
        ),
    )(sens)


def total_of(part):
    return jnp.sum(jnp.sum(part, axis=0, keepdims=True), axis=1, keepdims=True)


def step_kernel(idx_ref, f_ref, q_ref, tile_hbm, p_ref, coef_ref, dot_ref, tile_ref, acc_ref, sem):
    copy = pltpu.make_async_copy(tile_hbm, tile_ref, sem)
    copy.start()
    zeros = tuple(jnp.zeros((16, BS), jnp.float32) for _ in range(6))

    def at(d, k):
        return pl.ds(pl.multiple_of(d * 48 + 16 * k, 16), 16)

    def first(d, carry):
        out = []
        for k in range(3):
            f, q = f_ref[at(d, k), :], q_ref[at(d, k), :]
            out += [carry[2 * k] + f * f, carry[2 * k + 1] + f * q]
        return tuple(out)

    sums = lax.fori_loop(0, 128, first, zeros, unroll=4)
    now = [total_of(sums[2 * k]) for k in range(3)]
    alpha = [now[k] / total_of(sums[2 * k + 1]) for k in range(3)]

    def second(d, carry):
        out = []
        for k in range(3):
            r = f_ref[at(d, k), :] - alpha[k] * q_ref[at(d, k), :]
            p_ref[at(d, k), :] = r
            out.append(carry[k] + r * r)
        return tuple(out)

    sums = lax.fori_loop(0, 128, second, zeros[:3], unroll=4)
    later = [total_of(sums[k]) for k in range(3)]
    beta = [later[k] / now[k] for k in range(3)]

    def third(d, carry):
        for k in range(3):
            p_ref[at(d, k), :] = p_ref[at(d, k), :] + beta[k] * f_ref[at(d, k), :]
        return carry

    lax.fori_loop(0, 128, third, 0, unroll=4)
    rows = lax.broadcasted_iota(jnp.int32, (8, BS), 0)
    out = jnp.zeros((8, BS), jnp.float32)
    for k in range(3):
        out = jnp.where(rows == k, alpha[k], out)
        out = jnp.where(rows == 4 + k, later[k], out)
    coef_ref[...] = out
    copy.wait()
    sums = operator_sums(tile_ref, acc_ref, lambda n, k: p_ref[pl.ds(idx_ref[n] + 16 * k, 1), :])
    lanes = lax.broadcasted_iota(jnp.int32, (1, BS), 1)
    out = jnp.zeros((1, BS), jnp.float32)
    for k in range(3):
        total = jnp.zeros((1, BS), jnp.float32)
        for g in range(16):
            own = p_ref[pl.ds(idx_ref[9 * g] + 16 * k, 1), :]
            total = total + own * (own + sums[k][g] * COUPLING)
        out = jnp.where(lanes == k, jnp.sum(total, axis=1, keepdims=True), out)
    dot_ref[...] = out


def step_and_apply(idx, f, q, tiles):
    vmem = pl.BlockSpec(memory_space=pltpu.VMEM)
    return pl.pallas_call(
        step_kernel,
        out_shape=[
            jax.ShapeDtypeStruct(f.shape, jnp.float32),
            jax.ShapeDtypeStruct((8, BS), jnp.float32),
            jax.ShapeDtypeStruct((1, BS), jnp.float32),
        ],
        in_specs=[pl.BlockSpec(memory_space=pltpu.SMEM), vmem, vmem, pl.BlockSpec(memory_space=pl.ANY)],
        scratch_shapes=OPERATOR_SCRATCH,
        input_output_aliases={2: 0},
        compiler_params=pltpu.CompilerParams(vmem_limit_bytes=VMEM),
        cost_estimate=pl.CostEstimate(
            flops=f.size * 10 + tiles.size * 6, bytes_accessed=tiles.size * 8, transcendentals=0
        ),
    )(idx, f, q, tiles)


def copies(x):
    return jnp.broadcast_to(x[None], (lax.axis_size("ctl"),) + x.shape)


def over_ctl(x):
    return lax.all_to_all(x, "ctl", 0, 0, tiled=True)


def over_vol(x):
    return lax.all_gather(x, "vol", axis=0, tiled=True)


def place(block):
    return (((block >> 4) & 7) * 16 + (block >> 7)) * 48 + (block & 15)


def slot(block):
    return (((block >> 4) & 7) * 16 + (block >> 7)) * 16 + (block & 15)


def padded(rows):
    return jnp.pad(rows.transpose(1, 0, 2), ((0, 0), (0, 5), (0, 0)))


def body(sensitivity, sens_ids, ctl_coords, partners, node_coords, node_tiles):
    vol, ctl = lax.axis_index("vol"), lax.axis_index("ctl")
    device = vol * 16 + ctl
    blocks = ctl_coords.reshape(3, 128, BS)
    own_coords = lax.dynamic_slice_in_dim(blocks, vol * 16, 16, 1)
    ids = slot(sens_ids).astype(jnp.float32)
    lanes = jnp.arange(BS) // 16 == device % 8
    id_row = jnp.where(lanes, jnp.tile(ids, 8), 0.0)[None]
    payload = jnp.concatenate(
        [sensitivity.reshape(48, BS), jnp.pad(id_row, ((0, 7), (0, 0)))], axis=0
    )
    core = vol % 2
    half = lax.dynamic_slice_in_dim(blocks, core * 64, 64, 1).reshape(192, BS)
    near, half = lax.optimization_barrier((over_ctl(copies(payload)), copies(half)))
    sens = over_vol(near)
    half = over_ctl(half)
    other = lax.ppermute(half, "vol", [(i, i ^ 1) for i in range(lax.axis_size("vol"))])
    coords_rows = jnp.concatenate([half, other], axis=0).reshape(2 * 16 * 192, BS)

    own = ctl * 128 + vol * 16 + jnp.arange(16, dtype=jnp.int32)
    mates = lax.dynamic_slice_in_dim(partners, vol * 16, 16, 0)
    lists = jnp.concatenate([own[:, None], mates], axis=1).reshape(-1)
    node_lists = node_tiles.reshape(-1)
    op_at = place(lists)
    node_at = place(node_lists)

    def coord_at(block):
        return ((((block >> 6) & 1) ^ core) * 16 + (block >> 7)) * 192 + (block & 63)

    op_tiles = make_tiles(coord_at(lists), padded(own_coords), coords_rows, 9, 4)
    points = padded(node_coords.reshape(3, 64, BS))
    want = jnp.broadcast_to(slot(lists).astype(jnp.float32)[:, None], (144, BS))
    f_own, image = spread_and_apply(want, sens, op_tiles)
    image, sens = lax.optimization_barrier((copies(image), sens))
    near_image = over_ctl(image)
    f_all = spread_all(sens)
    near_image, f_all, coords_rows = lax.optimization_barrier((near_image, f_all, coords_rows))
    image_all = over_vol(near_image).reshape(128 * 48, BS)
    f_rows = f_all.reshape(128 * 48, BS)
    tiles = make_tiles(coord_at(node_lists), points, coords_rows, 9, 8)
    image_all, tiles = lax.optimization_barrier((image_all, tiles))
    p_rows, coef, dot_row = step_and_apply(op_at, f_rows, image_all, op_tiles)

    def mine(full):
        part = lax.dynamic_slice_in_dim(full.reshape(8, 16, 3, 16, BS), ctl, 1, 1)
        return part.reshape(8, 3, 16, BS).transpose(1, 0, 2, 3).reshape(3, 128, BS)

    f_mine, p_mine = mine(f_rows), mine(p_rows)
    alpha0 = coef[0:3, 0]
    dot_rows, p_rows, f_mine, p_mine = lax.optimization_barrier(
        (jnp.broadcast_to(dot_row[None], (128, 8, BS)), p_rows, f_mine, p_mine)
    )
    dot_rows = lax.all_to_all(dot_rows, ("vol", "ctl"), 0, 0, tiled=True)
    node_f, node_p = apply_tiles(node_at, tiles, [f_rows, p_rows], 9, 8)
    dot_rows, node_f, node_p = lax.optimization_barrier((dot_rows, node_f, node_p))
    alpha1 = coef[4:7, 0] / jnp.sum(dot_rows[:, 0], axis=0)[:3]

    def back(sums):
        return sums[:, :3].transpose(1, 0, 2)

    weights = alpha0[:, None, None] * f_mine + alpha1[:, None, None] * p_mine
    shift = NODE_SCALE * (
        alpha0[:, None, None] * back(node_f) + alpha1[:, None, None] * back(node_p)
    )
    return weights.reshape(3, -1), shift.reshape(3, -1)


def solution(mesh):
    placed = (
        P(None, ("vol", "ctl")),
        P(("vol", "ctl")),
        P(None, "ctl"),
        P("ctl", None),
        P(None, ("vol", "ctl")),
        P(("vol", "ctl"), None),
    )
    return jax.shard_map(
        body,
        mesh=mesh,
        in_specs=placed,
        out_specs=(P(None, "ctl"), P(None, ("vol", "ctl"))),
        check_vma=False,
    )
```

```python
import functools

import jax
import jax.numpy as jnp
from jax import lax
from jax.experimental import pallas as pl
from jax.experimental.pallas import tpu as pltpu
from jax.sharding import PartitionSpec as P

BS = 128
COUPLING = 0.0625
NODE_SCALE = 0.25
VMEM = 56 * 1024 * 1024
CHUNK = 32
STORED = 56
UNROLL = 7


def whole(shape):
    return pl.BlockSpec(shape, lambda *a: (0,) * len(shape))


def lane_sums(group, acc_ref):
    return [
        [
            jnp.sum(jnp.transpose(acc_ref[k, g * BS : (g + 1) * BS, :]), axis=0, keepdims=True)
            for g in range(group)
        ]
        for k in range(3)
    ]


def phi_block(g, base, reach, idx_ref, cols_ref, ctl_ref, tile_ref):
    for lo in range(0, BS, CHUNK):
        own = [
            jnp.broadcast_to(cols_ref[g, lo : lo + CHUNK, k : k + 1], (CHUNK, BS)) for k in range(3)
        ]
        for t in range(reach):
            at = idx_ref[base + t]
            dist = None
            for k in range(3):
                gap = own[k] - ctl_ref[pl.ds(at + 64 * k, 1), :]
                dist = gap * gap if dist is None else dist + gap * gap
            ratio = dist * lax.rsqrt(jnp.maximum(dist, 1e-30))
            inner = jnp.maximum(1.0 - ratio, 0.0)
            sq = inner * inner
            tile_ref[g * reach + t, lo : lo + CHUNK, :] = (sq * sq) * (4.0 * ratio + 1.0)


def tiles_kernel(reach, group, idx_ref, pts_ref, ctl_ref, tile_ref, cols_ref):
    step = pl.program_id(0)
    for g in range(group):
        cols_ref[g] = jnp.transpose(pts_ref[g])

    def one(g, carry):
        phi_block(g, (step * group + g) * reach, reach, idx_ref, cols_ref, ctl_ref, tile_ref)
        return carry

    lax.fori_loop(0, group, one, 0)


def make_tiles(idx, pts, ctl, reach, group):
    count = pts.shape[0]
    in_specs = [pl.BlockSpec((group, 8, BS), lambda m, *_: (m, 0, 0)), whole(ctl.shape)]
    elements = count * reach * BS * BS
    return pl.pallas_call(
        functools.partial(tiles_kernel, reach, group),
        out_shape=jax.ShapeDtypeStruct((count * reach, BS, BS), jnp.float32),
        grid_spec=pltpu.PrefetchScalarGridSpec(
            num_scalar_prefetch=1,
            grid=(count // group,),
            in_specs=in_specs,
            out_specs=pl.BlockSpec((group * reach, BS, BS), lambda m, *_: (m, 0, 0)),
            scratch_shapes=[pltpu.VMEM((group, BS, 8), jnp.float32)],
        ),
        compiler_params=pltpu.CompilerParams(vmem_limit_bytes=VMEM),
        cost_estimate=pl.CostEstimate(
            flops=elements * 24, bytes_accessed=elements * 4, transcendentals=elements
        ),
    )(idx, pts, ctl)


def node_kernel(
    reach, stored, fresh, total, idx_ref, at_ref, tile_ref, f_ref, p_ref, pts_ref, ctl_ref,
    sum_ref, more_ref, new_ref, cols_ref, rows_ref, raw_ref,
):
    step = pl.program_id(0)
    for g in range(fresh):
        cols_ref[g] = jnp.transpose(pts_ref[g])
    rows_ref[...] = jnp.zeros_like(rows_ref)

    def first(g):
        return jnp.where(g < stored, step * stored + g, total + step * fresh + g - stored) * reach

    def fill(g, carry):
        base = first(g)
        for t in range(reach):
            at = idx_ref[base + t]
            for k in range(3):
                rows_ref[g, k : k + 1, t * BS : (t + 1) * BS] = f_ref[pl.ds(at + 16 * k, 1), :]
                rows_ref[g, k + 3 : k + 4, t * BS : (t + 1) * BS] = p_ref[pl.ds(at + 16 * k, 1), :]
        return carry

    lax.fori_loop(0, stored + fresh, fill, 0)

    def apply(src_ref, g, slot):
        rows = rows_ref[slot]
        high = rows.astype(jnp.bfloat16).astype(jnp.float32)
        cut = jnp.concatenate([high, rows - high], axis=0).astype(jnp.bfloat16)
        tile = jnp.concatenate([src_ref[g * reach + t] for t in range(reach)], axis=1)
        high = tile.astype(jnp.bfloat16)
        rest = (tile - high.astype(jnp.float32)).astype(jnp.bfloat16)
        dims = (((1,), (1,)), ((), ()))
        out = lax.dot_general(high, cut, dims, preferred_element_type=jnp.float32)
        raw_ref[slot] = out + lax.dot_general(rest, cut, dims, preferred_element_type=jnp.float32)

    def old(g, carry):
        apply(tile_ref, g, g)
        return carry

    def make(g, carry):
        phi_block(
            g, (total + step * fresh + g) * reach, reach, at_ref, cols_ref, ctl_ref, new_ref
        )
        return carry

    lax.fori_loop(0, stored, old, 0, unroll=UNROLL)
    if fresh:
        lax.fori_loop(0, fresh, make, 0)
        for g in range(fresh):
            apply(new_ref, g, stored + g)
    for g in range(stored + fresh):
        both = jnp.transpose(raw_ref[g])
        both = both[:8] + both[8:]
        if g < stored:
            sum_ref[g] = both
        else:
            more_ref[g - stored] = both


def node_sums(idx, at, tiles, f, p, pts, ctl, reach, steps):
    total, extra = tiles.shape[0] // reach, pts.shape[0]
    stored, fresh = total // steps, extra // steps
    elements = (total + extra) * reach * BS * BS

    def block(count):
        return pl.BlockSpec((count, 8, BS), lambda m, *_: (m, 0, 0))

    return pl.pallas_call(
        functools.partial(node_kernel, reach, stored, fresh, total),
        out_shape=[
            jax.ShapeDtypeStruct((total, 8, BS), jnp.float32),
            jax.ShapeDtypeStruct((extra, 8, BS), jnp.float32),
        ],
        grid_spec=pltpu.PrefetchScalarGridSpec(
            num_scalar_prefetch=2,
            grid=(steps,),
            in_specs=[
                pl.BlockSpec((stored * reach, BS, BS), lambda m, *_: (m, 0, 0)),
                whole(f.shape),
                whole(p.shape),
                block(fresh),
                whole(ctl.shape),
            ],
            out_specs=[block(stored), block(fresh)],
            scratch_shapes=[
                pltpu.VMEM((fresh * reach, BS, BS), jnp.float32),
                pltpu.VMEM((fresh, BS, 8), jnp.float32),
                pltpu.VMEM((stored + fresh, 8, reach * BS), jnp.float32),
                pltpu.VMEM((stored + fresh, BS, 16), jnp.float32),
            ],
        ),
        compiler_params=pltpu.CompilerParams(vmem_limit_bytes=VMEM),
        cost_estimate=pl.CostEstimate(
            flops=elements * 12, bytes_accessed=elements * 4, transcendentals=0
        ),
    )(idx, at, tiles, f, p, pts, ctl)


def operator_sums(tile_ref, acc_ref, row):
    def one(g, carry):
        start = pl.multiple_of(g * BS, BS)
        for lo in range(0, BS, CHUNK):
            acc = [jnp.zeros((CHUNK, BS), jnp.float32) for _ in range(3)]
            for t in range(9):
                tile = tile_ref[g * 9 + t, lo : lo + CHUNK, :]
                for k in range(3):
                    part = row(g * 9 + t, k)
                    acc[k] = acc[k] + tile * (part * 8.0 if t == 0 else part)
            for k in range(3):
                acc_ref[k, pl.ds(start + lo, CHUNK), :] = acc[k]
        return carry

    lax.fori_loop(0, 16, one, 0)
    return lane_sums(16, acc_ref)


OPERATOR_SCRATCH = [
    pltpu.VMEM((144, BS, BS), jnp.float32),
    pltpu.VMEM((3, 16 * BS, BS), jnp.float32),
    pltpu.SemaphoreType.DMA,
]


def spread_kernel(want_ref, sens_ref, tile_hbm, own_ref, image_ref, near_ref, tile_ref, acc_ref, sem):
    copy = pltpu.make_async_copy(tile_hbm, tile_ref, sem)
    copy.start()
    ids = jnp.sum(sens_ref[:, 48, :].reshape(16, 8, BS), axis=1)
    want = want_ref[...]
    acc = [jnp.zeros((144, BS), jnp.float32) for _ in range(3)]
    for g in range(16):
        hot = (want == ids[g : g + 1, :]).astype(jnp.bfloat16)
        for k in range(3):
            part = sens_ref[8 * g : 8 * g + 8, 16 * k : 16 * k + 16, :].reshape(BS, BS)
            high = part.astype(jnp.bfloat16)
            rest = (part - high.astype(jnp.float32)).astype(jnp.bfloat16)
            acc[k] = acc[k] + jnp.dot(hot, high, preferred_element_type=jnp.float32)
            acc[k] = acc[k] + jnp.dot(hot, rest, preferred_element_type=jnp.float32)
    for k in range(3):
        near_ref[144 * k : 144 * k + 144] = acc[k]
    copy.wait()
    sums = operator_sums(tile_ref, acc_ref, lambda n, k: near_ref[pl.ds(n + 144 * k, 1), :])
    for k in range(3):
        for g in range(16):
            own = near_ref[144 * k + 9 * g : 144 * k + 9 * g + 1, :]
            own_ref[16 * k + g : 16 * k + g + 1, :] = own
            image_ref[16 * k + g : 16 * k + g + 1, :] = own + sums[k][g] * COUPLING


def spread_and_apply(want, sens, tiles):
    return pl.pallas_call(
        spread_kernel,
        out_shape=[jax.ShapeDtypeStruct((48, BS), jnp.float32)] * 2,
        in_specs=[
            pl.BlockSpec(memory_space=pltpu.VMEM),
            pl.BlockSpec(memory_space=pltpu.VMEM),
            pl.BlockSpec(memory_space=pl.ANY),
        ],
        scratch_shapes=[pltpu.VMEM((3 * 144, BS), jnp.float32)] + OPERATOR_SCRATCH,
        compiler_params=pltpu.CompilerParams(vmem_limit_bytes=VMEM),
        cost_estimate=pl.CostEstimate(
            flops=144 * 2048 * 384 * 4, bytes_accessed=tiles.size * 4, transcendentals=0
        ),
    )(want, sens, tiles)


def spread_all_kernel(sens_ref, out_ref, cut_ref, ids_ref):
    step = pl.program_id(0)

    @pl.when(step == 0)
    def _():
        ids_ref[...] = jnp.sum(sens_ref[:, 48, :].reshape(16, 8, BS), axis=1)
        for k in range(3):
            part = sens_ref[:, 16 * k : 16 * k + 16, :].reshape(2048, BS)
            high = part.astype(jnp.bfloat16)
            cut_ref[:, k * BS : (k + 1) * BS] = high
            cut_ref[:, (k + 3) * BS : (k + 4) * BS] = (part - high.astype(jnp.float32)).astype(jnp.bfloat16)

    want = (lax.broadcasted_iota(jnp.int32, (256, BS), 0) + step * 256).astype(jnp.float32)
    hot = jnp.concatenate(
        [(want == ids_ref[g : g + 1, :]).astype(jnp.bfloat16) for g in range(16)], axis=1
    )
    acc = jnp.dot(hot, cut_ref[...], preferred_element_type=jnp.float32)
    acc = acc[:, : 3 * BS] + acc[:, 3 * BS :]
    for k in range(3):
        out_ref[:, 16 * k : 16 * k + 16, :] = acc[:, k * BS : (k + 1) * BS].reshape(16, 16, BS)


def spread_all(sens):
    return pl.pallas_call(
        spread_all_kernel,
        out_shape=jax.ShapeDtypeStruct((128, 48, BS), jnp.float32),
        grid=(8,),
        in_specs=[whole(sens.shape)],
        out_specs=pl.BlockSpec((16, 48, BS), lambda m: (m, 0, 0)),
        scratch_shapes=[
            pltpu.VMEM((2048, 6 * BS), jnp.bfloat16),
            pltpu.VMEM((16, BS), jnp.float32),
        ],
        compiler_params=pltpu.CompilerParams(vmem_limit_bytes=VMEM),
        cost_estimate=pl.CostEstimate(
            flops=2048 * 2048 * 384 * 4, bytes_accessed=sens.size * 8, transcendentals=0
        ),
    )(sens)


def total_of(part):
    return jnp.sum(jnp.sum(part, axis=0, keepdims=True), axis=1, keepdims=True)


def step_kernel(idx_ref, f_ref, q_ref, tile_hbm, p_ref, coef_ref, dot_ref, tile_ref, acc_ref, sem):
    copy = pltpu.make_async_copy(tile_hbm, tile_ref, sem)
    copy.start()
    zeros = tuple(jnp.zeros((16, BS), jnp.float32) for _ in range(6))

    def at(d, k):
        return pl.ds(pl.multiple_of(d * 48 + 16 * k, 16), 16)

    def first(d, carry):
        out = []
        for k in range(3):
            f, q = f_ref[at(d, k), :], q_ref[at(d, k), :]
            out += [carry[2 * k] + f * f, carry[2 * k + 1] + f * q]
        return tuple(out)

    sums = lax.fori_loop(0, 128, first, zeros, unroll=4)
    now = [total_of(sums[2 * k]) for k in range(3)]
    alpha = [now[k] / total_of(sums[2 * k + 1]) for k in range(3)]

    def second(d, carry):
        out = []
        for k in range(3):
            r = f_ref[at(d, k), :] - alpha[k] * q_ref[at(d, k), :]
            p_ref[at(d, k), :] = r
            out.append(carry[k] + r * r)
        return tuple(out)

    sums = lax.fori_loop(0, 128, second, zeros[:3], unroll=4)
    later = [total_of(sums[k]) for k in range(3)]
    beta = [later[k] / now[k] for k in range(3)]

    def third(d, carry):
        for k in range(3):
            p_ref[at(d, k), :] = p_ref[at(d, k), :] + beta[k] * f_ref[at(d, k), :]
        return carry

    lax.fori_loop(0, 128, third, 0, unroll=4)
    rows = lax.broadcasted_iota(jnp.int32, (8, BS), 0)
    out = jnp.zeros((8, BS), jnp.float32)
    for k in range(3):
        out = jnp.where(rows == k, alpha[k], out)
        out = jnp.where(rows == 4 + k, later[k], out)
    coef_ref[...] = out
    copy.wait()
    sums = operator_sums(tile_ref, acc_ref, lambda n, k: p_ref[pl.ds(idx_ref[n] + 16 * k, 1), :])
    lanes = lax.broadcasted_iota(jnp.int32, (1, BS), 1)
    out = jnp.zeros((1, BS), jnp.float32)
    for k in range(3):
        total = jnp.zeros((1, BS), jnp.float32)
        for g in range(16):
            own = p_ref[pl.ds(idx_ref[9 * g] + 16 * k, 1), :]
            total = total + own * (own + sums[k][g] * COUPLING)
        out = jnp.where(lanes == k, jnp.sum(total, axis=1, keepdims=True), out)
    dot_ref[...] = out


def step_and_apply(idx, f, q, tiles):
    vmem = pl.BlockSpec(memory_space=pltpu.VMEM)
    return pl.pallas_call(
        step_kernel,
        out_shape=[
            jax.ShapeDtypeStruct(f.shape, jnp.float32),
            jax.ShapeDtypeStruct((8, BS), jnp.float32),
            jax.ShapeDtypeStruct((1, BS), jnp.float32),
        ],
        in_specs=[pl.BlockSpec(memory_space=pltpu.SMEM), vmem, vmem, pl.BlockSpec(memory_space=pl.ANY)],
        scratch_shapes=OPERATOR_SCRATCH,
        input_output_aliases={2: 0},
        compiler_params=pltpu.CompilerParams(vmem_limit_bytes=VMEM),
        cost_estimate=pl.CostEstimate(
            flops=f.size * 10 + tiles.size * 6, bytes_accessed=tiles.size * 8, transcendentals=0
        ),
    )(idx, f, q, tiles)


def copies(x):
    return jnp.broadcast_to(x[None], (lax.axis_size("ctl"),) + x.shape)


def over_ctl(x):
    return lax.all_to_all(x, "ctl", 0, 0, tiled=True)


def over_vol(x):
    return lax.all_gather(x, "vol", axis=0, tiled=True)


def place(block):
    return (((block >> 4) & 7) * 16 + (block >> 7)) * 48 + (block & 15)


def slot(block):
    return (((block >> 4) & 7) * 16 + (block >> 7)) * 16 + (block & 15)


def padded(rows):
    return jnp.pad(rows.transpose(1, 0, 2), ((0, 0), (0, 5), (0, 0)))


def body(sensitivity, sens_ids, ctl_coords, partners, node_coords, node_tiles):
    vol, ctl = lax.axis_index("vol"), lax.axis_index("ctl")
    device = vol * 16 + ctl
    blocks = ctl_coords.reshape(3, 128, BS)
    own_coords = lax.dynamic_slice_in_dim(blocks, vol * 16, 16, 1)
    ids = slot(sens_ids).astype(jnp.float32)
    lanes = jnp.arange(BS) // 16 == device % 8
    id_row = jnp.where(lanes, jnp.tile(ids, 8), 0.0)[None]
    payload = jnp.concatenate(
        [sensitivity.reshape(48, BS), jnp.pad(id_row, ((0, 7), (0, 0)))], axis=0
    )
    core = vol % 2
    half = lax.dynamic_slice_in_dim(blocks, core * 64, 64, 1).reshape(192, BS)
    near, half = lax.optimization_barrier((over_ctl(copies(payload)), copies(half)))
    sens = over_vol(near)
    half = over_ctl(half)
    other = lax.ppermute(half, "vol", [(i, i ^ 1) for i in range(lax.axis_size("vol"))])
    coords_rows = jnp.concatenate([half, other], axis=0).reshape(2 * 16 * 192, BS)

    own = ctl * 128 + vol * 16 + jnp.arange(16, dtype=jnp.int32)
    mates = lax.dynamic_slice_in_dim(partners, vol * 16, 16, 0)
    lists = jnp.concatenate([own[:, None], mates], axis=1).reshape(-1)
    node_lists = node_tiles.reshape(-1)
    op_at = place(lists)
    node_at = place(node_lists)

    def coord_at(block):
        return ((((block >> 6) & 1) ^ core) * 16 + (block >> 7)) * 192 + (block & 63)

    op_tiles = make_tiles(coord_at(lists), padded(own_coords), coords_rows, 9, 4)
    points = padded(node_coords.reshape(3, 64, BS))
    want = jnp.broadcast_to(slot(lists).astype(jnp.float32)[:, None], (144, BS))
    f_own, image = spread_and_apply(want, sens, op_tiles)
    image, sens = lax.optimization_barrier((copies(image), sens))
    near_image = over_ctl(image)
    f_all = spread_all(sens)
    near_image, f_all, coords_rows = lax.optimization_barrier((near_image, f_all, coords_rows))
    image_all = over_vol(near_image).reshape(128 * 48, BS)
    f_rows = f_all.reshape(128 * 48, BS)
    tiles = make_tiles(coord_at(node_lists), points[:STORED], coords_rows, 9, 8)
    image_all, tiles = lax.optimization_barrier((image_all, tiles))
    p_rows, coef, dot_row = step_and_apply(op_at, f_rows, image_all, op_tiles)

    def mine(full):
        part = lax.dynamic_slice_in_dim(full.reshape(8, 16, 3, 16, BS), ctl, 1, 1)
        return part.reshape(8, 3, 16, BS).transpose(1, 0, 2, 3).reshape(3, 128, BS)

    f_mine, p_mine = mine(f_rows), mine(p_rows)
    alpha0 = coef[0:3, 0]
    dot_rows, p_rows, f_mine, p_mine = lax.optimization_barrier(
        (jnp.broadcast_to(dot_row[None], (128, 8, BS)), p_rows, f_mine, p_mine)
    )
    dot_rows = lax.all_to_all(dot_rows, ("vol", "ctl"), 0, 0, tiled=True)
    sums, more = node_sums(
        node_at, coord_at(node_lists), tiles, f_rows, p_rows, points[STORED:], coords_rows, 9, 8
    )
    dot_rows, sums, more = lax.optimization_barrier((dot_rows, sums, more))
    sums = jnp.concatenate([sums, more], axis=0).transpose(1, 0, 2)
    alpha1 = coef[4:7, 0] / jnp.sum(dot_rows[:, 0], axis=0)[:3]

    weights = alpha0[:, None, None] * f_mine + alpha1[:, None, None] * p_mine
    shift = NODE_SCALE * (
        alpha0[:, None, None] * sums[0:3] + alpha1[:, None, None] * sums[3:6]
    )
    return weights.reshape(3, -1), shift.reshape(3, -1)


def solution(mesh):
    placed = (
        P(None, ("vol", "ctl")),
        P(("vol", "ctl")),
        P(None, "ctl"),
        P("ctl", None),
        P(None, ("vol", "ctl")),
        P(("vol", "ctl"), None),
    )
    return jax.shard_map(
        body,
        mesh=mesh,
        in_specs=placed,
        out_specs=(P(None, "ctl"), P(None, ("vol", "ctl"))),
        check_vma=False,
    )
```

```python
import functools

import jax
import jax.numpy as jnp
from jax import lax
from jax.experimental import pallas as pl
from jax.experimental.pallas import tpu as pltpu
from jax.sharding import PartitionSpec as P

BS = 128
COUPLING = 0.0625
NODE_SCALE = 0.25
VMEM = 56 * 1024 * 1024
CHUNK = 32
STORED = 56
UNROLL = 7


def whole(shape):
    return pl.BlockSpec(shape, lambda *a: (0,) * len(shape))


def lane_sums(group, acc_ref):
    return [
        [
            jnp.sum(jnp.transpose(acc_ref[k, g * BS : (g + 1) * BS, :]), axis=0, keepdims=True)
            for g in range(group)
        ]
        for k in range(3)
    ]


def phi_block(g, base, reach, idx_ref, cols_ref, ctl_ref, tile_ref):
    for lo in range(0, BS, CHUNK):
        own = [
            jnp.broadcast_to(cols_ref[g, lo : lo + CHUNK, k : k + 1], (CHUNK, BS)) for k in range(3)
        ]
        for t in range(reach):
            at = idx_ref[base + t]
            dist = None
            for k in range(3):
                gap = own[k] - ctl_ref[pl.ds(at + 64 * k, 1), :]
                dist = gap * gap if dist is None else dist + gap * gap
            ratio = dist * lax.rsqrt(jnp.maximum(dist, 1e-30))
            inner = jnp.maximum(1.0 - ratio, 0.0)
            sq = inner * inner
            tile_ref[g * reach + t, lo : lo + CHUNK, :] = (sq * sq) * (4.0 * ratio + 1.0)


def tiles_kernel(reach, group, idx_ref, pts_ref, ctl_ref, tile_ref, cols_ref):
    step = pl.program_id(0)
    for g in range(group):
        cols_ref[g] = jnp.transpose(pts_ref[g])

    def one(g, carry):
        phi_block(g, (step * group + g) * reach, reach, idx_ref, cols_ref, ctl_ref, tile_ref)
        return carry

    lax.fori_loop(0, group, one, 0)


def make_tiles(idx, pts, ctl, reach, group):
    count = pts.shape[0]
    in_specs = [pl.BlockSpec((group, 8, BS), lambda m, *_: (m, 0, 0)), whole(ctl.shape)]
    elements = count * reach * BS * BS
    return pl.pallas_call(
        functools.partial(tiles_kernel, reach, group),
        out_shape=jax.ShapeDtypeStruct((count * reach, BS, BS), jnp.float32),
        grid_spec=pltpu.PrefetchScalarGridSpec(
            num_scalar_prefetch=1,
            grid=(count // group,),
            in_specs=in_specs,
            out_specs=pl.BlockSpec((group * reach, BS, BS), lambda m, *_: (m, 0, 0)),
            scratch_shapes=[pltpu.VMEM((group, BS, 8), jnp.float32)],
        ),
        compiler_params=pltpu.CompilerParams(vmem_limit_bytes=VMEM),
        cost_estimate=pl.CostEstimate(
            flops=elements * 24, bytes_accessed=elements * 4, transcendentals=elements
        ),
    )(idx, pts, ctl)


def node_kernel(
    reach, stored, fresh, total, idx_ref, at_ref, tile_ref, f_ref, p_ref, pts_ref, ctl_ref,
    sum_ref, more_ref, new_ref, cols_ref, rows_ref, raw_ref,
):
    step = pl.program_id(0)
    for g in range(fresh):
        cols_ref[g] = jnp.transpose(pts_ref[g])
    rows_ref[...] = jnp.zeros_like(rows_ref)

    def first(g):
        return jnp.where(g < stored, step * stored + g, total + step * fresh + g - stored) * reach

    def fill(g, carry):
        base = first(g)
        for t in range(reach):
            at = idx_ref[base + t]
            for k in range(3):
                rows_ref[g, k : k + 1, t * BS : (t + 1) * BS] = f_ref[pl.ds(at + 16 * k, 1), :]
                rows_ref[g, k + 3 : k + 4, t * BS : (t + 1) * BS] = p_ref[pl.ds(at + 16 * k, 1), :]
        return carry

    lax.fori_loop(0, stored + fresh, fill, 0)

    def apply(src_ref, g, slot):
        rows = rows_ref[slot]
        high = rows.astype(jnp.bfloat16).astype(jnp.float32)
        cut = jnp.concatenate([high, rows - high], axis=0).astype(jnp.bfloat16)
        tile = jnp.concatenate([src_ref[g * reach + t] for t in range(reach)], axis=1)
        high = tile.astype(jnp.bfloat16)
        rest = (tile - high.astype(jnp.float32)).astype(jnp.bfloat16)
        dims = (((1,), (1,)), ((), ()))
        out = lax.dot_general(high, cut, dims, preferred_element_type=jnp.float32)
        raw_ref[slot] = out + lax.dot_general(rest, cut, dims, preferred_element_type=jnp.float32)

    def old(g, carry):
        apply(tile_ref, g, g)
        return carry

    def make(g, carry):
        phi_block(
            g, (total + step * fresh + g) * reach, reach, at_ref, cols_ref, ctl_ref, new_ref
        )
        return carry

    lax.fori_loop(0, stored, old, 0, unroll=UNROLL)
    if fresh:
        lax.fori_loop(0, fresh, make, 0)
        for g in range(fresh):
            apply(new_ref, g, stored + g)
    for g in range(stored + fresh):
        both = jnp.transpose(raw_ref[g])
        both = both[:8] + both[8:]
        if g < stored:
            sum_ref[g] = both
        else:
            more_ref[g - stored] = both


def node_sums(idx, at, tiles, f, p, pts, ctl, reach, steps):
    total, extra = tiles.shape[0] // reach, pts.shape[0]
    stored, fresh = total // steps, extra // steps
    elements = (total + extra) * reach * BS * BS

    def block(count):
        return pl.BlockSpec((count, 8, BS), lambda m, *_: (m, 0, 0))

    return pl.pallas_call(
        functools.partial(node_kernel, reach, stored, fresh, total),
        out_shape=[
            jax.ShapeDtypeStruct((total, 8, BS), jnp.float32),
            jax.ShapeDtypeStruct((extra, 8, BS), jnp.float32),
        ],
        grid_spec=pltpu.PrefetchScalarGridSpec(
            num_scalar_prefetch=2,
            grid=(steps,),
            in_specs=[
                pl.BlockSpec((stored * reach, BS, BS), lambda m, *_: (m, 0, 0)),
                whole(f.shape),
                whole(p.shape),
                block(fresh),
                whole(ctl.shape),
            ],
            out_specs=[block(stored), block(fresh)],
            scratch_shapes=[
                pltpu.VMEM((fresh * reach, BS, BS), jnp.float32),
                pltpu.VMEM((fresh, BS, 8), jnp.float32),
                pltpu.VMEM((stored + fresh, 8, reach * BS), jnp.float32),
                pltpu.VMEM((stored + fresh, BS, 16), jnp.float32),
            ],
        ),
        compiler_params=pltpu.CompilerParams(vmem_limit_bytes=VMEM),
        cost_estimate=pl.CostEstimate(
            flops=elements * 12, bytes_accessed=elements * 4, transcendentals=0
        ),
    )(idx, at, tiles, f, p, pts, ctl)


def operator_sums(tile_ref, acc_ref, row):
    def one(g, carry):
        start = pl.multiple_of(g * BS, BS)
        for lo in range(0, BS, CHUNK):
            acc = [jnp.zeros((CHUNK, BS), jnp.float32) for _ in range(3)]
            for t in range(9):
                tile = tile_ref[g * 9 + t, lo : lo + CHUNK, :]
                for k in range(3):
                    part = row(g * 9 + t, k)
                    acc[k] = acc[k] + tile * (part * 8.0 if t == 0 else part)
            for k in range(3):
                acc_ref[k, pl.ds(start + lo, CHUNK), :] = acc[k]
        return carry

    lax.fori_loop(0, 16, one, 0)
    return lane_sums(16, acc_ref)


OPERATOR_SCRATCH = [
    pltpu.VMEM((144, BS, BS), jnp.float32),
    pltpu.VMEM((3, 16 * BS, BS), jnp.float32),
    pltpu.SemaphoreType.DMA,
]


def spread_kernel(want_ref, sens_ref, tile_hbm, own_ref, image_ref, near_ref, tile_ref, acc_ref, sem):
    copy = pltpu.make_async_copy(tile_hbm, tile_ref, sem)
    copy.start()
    ids = jnp.sum(sens_ref[:, 48, :].reshape(16, 8, BS), axis=1)
    want = want_ref[...]
    acc = [jnp.zeros((144, BS), jnp.float32) for _ in range(3)]
    for g in range(16):
        hot = (want == ids[g : g + 1, :]).astype(jnp.bfloat16)
        for k in range(3):
            part = sens_ref[8 * g : 8 * g + 8, 16 * k : 16 * k + 16, :].reshape(BS, BS)
            high = part.astype(jnp.bfloat16)
            rest = (part - high.astype(jnp.float32)).astype(jnp.bfloat16)
            acc[k] = acc[k] + jnp.dot(hot, high, preferred_element_type=jnp.float32)
            acc[k] = acc[k] + jnp.dot(hot, rest, preferred_element_type=jnp.float32)
    for k in range(3):
        near_ref[144 * k : 144 * k + 144] = acc[k]
    copy.wait()
    sums = operator_sums(tile_ref, acc_ref, lambda n, k: near_ref[pl.ds(n + 144 * k, 1), :])
    for k in range(3):
        for g in range(16):
            own = near_ref[144 * k + 9 * g : 144 * k + 9 * g + 1, :]
            own_ref[16 * k + g : 16 * k + g + 1, :] = own
            image_ref[0, 16 * k + g : 16 * k + g + 1, :] = own + sums[k][g] * COUPLING
    for n in range(1, 16):
        image_ref[n] = image_ref[0]


def spread_and_apply(want, sens, tiles):
    return pl.pallas_call(
        spread_kernel,
        out_shape=[
            jax.ShapeDtypeStruct((48, BS), jnp.float32),
            jax.ShapeDtypeStruct((16, 48, BS), jnp.float32),
        ],
        in_specs=[
            pl.BlockSpec(memory_space=pltpu.VMEM),
            pl.BlockSpec(memory_space=pltpu.VMEM),
            pl.BlockSpec(memory_space=pl.ANY),
        ],
        scratch_shapes=[pltpu.VMEM((3 * 144, BS), jnp.float32)] + OPERATOR_SCRATCH,
        compiler_params=pltpu.CompilerParams(vmem_limit_bytes=VMEM),
        cost_estimate=pl.CostEstimate(
            flops=144 * 2048 * 384 * 4, bytes_accessed=tiles.size * 4, transcendentals=0
        ),
    )(want, sens, tiles)


def spread_all_kernel(sens_ref, out_ref, cut_ref, ids_ref):
    step = pl.program_id(0)

    @pl.when(step == 0)
    def _():
        ids_ref[...] = jnp.sum(sens_ref[:, 48, :].reshape(16, 8, BS), axis=1)
        for k in range(3):
            part = sens_ref[:, 16 * k : 16 * k + 16, :].reshape(2048, BS)
            high = part.astype(jnp.bfloat16)
            cut_ref[:, k * BS : (k + 1) * BS] = high
            cut_ref[:, (k + 3) * BS : (k + 4) * BS] = (part - high.astype(jnp.float32)).astype(jnp.bfloat16)

    want = (lax.broadcasted_iota(jnp.int32, (256, BS), 0) + step * 256).astype(jnp.float32)
    hot = jnp.concatenate(
        [(want == ids_ref[g : g + 1, :]).astype(jnp.bfloat16) for g in range(16)], axis=1
    )
    acc = jnp.dot(hot, cut_ref[...], preferred_element_type=jnp.float32)
    acc = acc[:, : 3 * BS] + acc[:, 3 * BS :]
    for k in range(3):
        out_ref[:, 16 * k : 16 * k + 16, :] = acc[:, k * BS : (k + 1) * BS].reshape(16, 16, BS)


def spread_all(sens):
    return pl.pallas_call(
        spread_all_kernel,
        out_shape=jax.ShapeDtypeStruct((128, 48, BS), jnp.float32),
        grid=(8,),
        in_specs=[whole(sens.shape)],
        out_specs=pl.BlockSpec((16, 48, BS), lambda m: (m, 0, 0)),
        scratch_shapes=[
            pltpu.VMEM((2048, 6 * BS), jnp.bfloat16),
            pltpu.VMEM((16, BS), jnp.float32),
        ],
        compiler_params=pltpu.CompilerParams(vmem_limit_bytes=VMEM),
        cost_estimate=pl.CostEstimate(
            flops=2048 * 2048 * 384 * 4, bytes_accessed=sens.size * 8, transcendentals=0
        ),
    )(sens)


def total_of(part):
    return jnp.sum(jnp.sum(part, axis=0, keepdims=True), axis=1, keepdims=True)


def step_kernel(idx_ref, f_ref, q_ref, tile_hbm, p_ref, coef_ref, dot_ref, tile_ref, acc_ref, sem):
    copy = pltpu.make_async_copy(tile_hbm, tile_ref, sem)
    copy.start()
    zeros = tuple(jnp.zeros((16, BS), jnp.float32) for _ in range(6))

    def at(d, k):
        return pl.ds(pl.multiple_of(d * 48 + 16 * k, 16), 16)

    def first(d, carry):
        out = []
        for k in range(3):
            f, q = f_ref[at(d, k), :], q_ref[at(d, k), :]
            out += [carry[2 * k] + f * f, carry[2 * k + 1] + f * q]
        return tuple(out)

    sums = lax.fori_loop(0, 128, first, zeros, unroll=4)
    now = [total_of(sums[2 * k]) for k in range(3)]
    alpha = [now[k] / total_of(sums[2 * k + 1]) for k in range(3)]

    def second(d, carry):
        out = []
        for k in range(3):
            r = f_ref[at(d, k), :] - alpha[k] * q_ref[at(d, k), :]
            p_ref[at(d, k), :] = r
            out.append(carry[k] + r * r)
        return tuple(out)

    sums = lax.fori_loop(0, 128, second, zeros[:3], unroll=4)
    later = [total_of(sums[k]) for k in range(3)]
    beta = [later[k] / now[k] for k in range(3)]

    def third(d, carry):
        for k in range(3):
            p_ref[at(d, k), :] = p_ref[at(d, k), :] + beta[k] * f_ref[at(d, k), :]
        return carry

    lax.fori_loop(0, 128, third, 0, unroll=4)
    rows = lax.broadcasted_iota(jnp.int32, (8, BS), 0)
    out = jnp.zeros((8, BS), jnp.float32)
    for k in range(3):
        out = jnp.where(rows == k, alpha[k], out)
        out = jnp.where(rows == 4 + k, later[k], out)
    coef_ref[...] = out
    copy.wait()
    sums = operator_sums(tile_ref, acc_ref, lambda n, k: p_ref[pl.ds(idx_ref[n] + 16 * k, 1), :])
    lanes = lax.broadcasted_iota(jnp.int32, (1, BS), 1)
    out = jnp.zeros((1, BS), jnp.float32)
    for k in range(3):
        total = jnp.zeros((1, BS), jnp.float32)
        for g in range(16):
            own = p_ref[pl.ds(idx_ref[9 * g] + 16 * k, 1), :]
            total = total + own * (own + sums[k][g] * COUPLING)
        out = jnp.where(lanes == k, jnp.sum(total, axis=1, keepdims=True), out)
    dot_ref[...] = jnp.broadcast_to(out[None], (128, 8, BS))


def step_and_apply(idx, f, q, tiles):
    vmem = pl.BlockSpec(memory_space=pltpu.VMEM)
    return pl.pallas_call(
        step_kernel,
        out_shape=[
            jax.ShapeDtypeStruct(f.shape, jnp.float32),
            jax.ShapeDtypeStruct((8, BS), jnp.float32),
            jax.ShapeDtypeStruct((128, 8, BS), jnp.float32),
        ],
        in_specs=[pl.BlockSpec(memory_space=pltpu.SMEM), vmem, vmem, pl.BlockSpec(memory_space=pl.ANY)],
        scratch_shapes=OPERATOR_SCRATCH,
        input_output_aliases={2: 0},
        compiler_params=pltpu.CompilerParams(vmem_limit_bytes=VMEM),
        cost_estimate=pl.CostEstimate(
            flops=f.size * 10 + tiles.size * 6, bytes_accessed=tiles.size * 8, transcendentals=0
        ),
    )(idx, f, q, tiles)


def copies(x):
    return jnp.broadcast_to(x[None], (lax.axis_size("ctl"),) + x.shape)


def over_ctl(x):
    return lax.all_to_all(x, "ctl", 0, 0, tiled=True)


def over_vol(x):
    return lax.all_gather(x, "vol", axis=0, tiled=True)


def place(block):
    return (((block >> 4) & 7) * 16 + (block >> 7)) * 48 + (block & 15)


def slot(block):
    return (((block >> 4) & 7) * 16 + (block >> 7)) * 16 + (block & 15)


def padded(rows):
    return jnp.pad(rows.transpose(1, 0, 2), ((0, 0), (0, 5), (0, 0)))


def body(sensitivity, sens_ids, ctl_coords, partners, node_coords, node_tiles):
    vol, ctl = lax.axis_index("vol"), lax.axis_index("ctl")
    device = vol * 16 + ctl
    blocks = ctl_coords.reshape(3, 128, BS)
    own_coords = lax.dynamic_slice_in_dim(blocks, vol * 16, 16, 1)
    ids = slot(sens_ids).astype(jnp.float32)
    lanes = jnp.arange(BS) // 16 == device % 8
    id_row = jnp.where(lanes, jnp.tile(ids, 8), 0.0)[None]
    payload = jnp.concatenate(
        [sensitivity.reshape(48, BS), jnp.pad(id_row, ((0, 7), (0, 0)))], axis=0
    )
    core = vol % 2
    own = ctl * 128 + vol * 16 + jnp.arange(16, dtype=jnp.int32)
    mates = lax.dynamic_slice_in_dim(partners, vol * 16, 16, 0)
    lists = jnp.concatenate([own[:, None], mates], axis=1).reshape(-1)
    node_lists = node_tiles.reshape(-1)

    def coord_at(block):
        return ((((block >> 6) & 1) ^ core) * 16 + (block >> 7)) * 192 + (block & 63)

    points = padded(node_coords.reshape(3, 64, BS))
    ready = (
        place(lists),
        place(node_lists),
        coord_at(lists),
        coord_at(node_lists),
        padded(own_coords),
        points[:STORED],
        points[STORED:],
        jnp.broadcast_to(slot(lists).astype(jnp.float32)[:, None], (144, BS)),
    )
    half = copies(lax.dynamic_slice_in_dim(blocks, core * 64, 64, 1).reshape(192, BS))
    sens = over_vol(over_ctl(copies(payload)))
    half = over_ctl(half)
    half, ready = lax.optimization_barrier((half, ready))
    op_at, node_at, op_coord_at, node_coord_at, own_points, points, more_points, want = ready
    other = lax.ppermute(half, "vol", [(i, i ^ 1) for i in range(lax.axis_size("vol"))])
    coords_rows = jnp.concatenate([half, other], axis=0).reshape(2 * 16 * 192, BS)
    op_tiles = make_tiles(op_coord_at, own_points, coords_rows, 9, 4)
    f_own, image = spread_and_apply(want, sens, op_tiles)
    image, sens = lax.optimization_barrier((image, sens))
    near_image = over_ctl(image)
    f_all = spread_all(sens)
    near_image, f_all, coords_rows = lax.optimization_barrier((near_image, f_all, coords_rows))
    image_all = over_vol(near_image).reshape(128 * 48, BS)
    f_rows = f_all.reshape(128 * 48, BS)
    tiles = make_tiles(node_coord_at, points, coords_rows, 9, 8)
    image_all, tiles = lax.optimization_barrier((image_all, tiles))
    p_rows, coef, dot_row = step_and_apply(op_at, f_rows, image_all, op_tiles)

    def mine(full):
        part = lax.dynamic_slice_in_dim(full.reshape(8, 16, 3, 16, BS), ctl, 1, 1)
        return part.reshape(8, 3, 16, BS).transpose(1, 0, 2, 3).reshape(3, 128, BS)

    f_mine, p_mine = mine(f_rows), mine(p_rows)
    alpha0 = coef[0:3, 0]
    dot_rows, p_rows, f_mine, p_mine = lax.optimization_barrier(
        (dot_row, p_rows, f_mine, p_mine)
    )
    dot_rows = lax.all_to_all(dot_rows, ("vol", "ctl"), 0, 0, tiled=True)
    sums, more = node_sums(
        node_at, node_coord_at, tiles, f_rows, p_rows, more_points, coords_rows, 9, 8
    )
    dot_rows, sums, more = lax.optimization_barrier((dot_rows, sums, more))
    sums = jnp.concatenate([sums, more], axis=0).transpose(1, 0, 2)
    alpha1 = coef[4:7, 0] / jnp.sum(dot_rows[:, 0], axis=0)[:3]

    weights = alpha0[:, None, None] * f_mine + alpha1[:, None, None] * p_mine
    shift = NODE_SCALE * (
        alpha0[:, None, None] * sums[0:3] + alpha1[:, None, None] * sums[3:6]
    )
    return weights.reshape(3, -1), shift.reshape(3, -1)


def solution(mesh):
    placed = (
        P(None, ("vol", "ctl")),
        P(("vol", "ctl")),
        P(None, "ctl"),
        P("ctl", None),
        P(None, ("vol", "ctl")),
        P(("vol", "ctl"), None),
    )
    return jax.shard_map(
        body,
        mesh=mesh,
        in_specs=placed,
        out_specs=(P(None, "ctl"), P(None, ("vol", "ctl"))),
        check_vma=False,
    )
```

```python
import functools

import jax
import jax.numpy as jnp
from jax import lax
from jax.experimental import pallas as pl
from jax.experimental.pallas import tpu as pltpu
from jax.sharding import PartitionSpec as P

BS = 128
COUPLING = 0.0625
NODE_SCALE = 0.25
VMEM = 56 * 1024 * 1024
CHUNK = 32
STORED = 56
UNROLL = 7


def whole(shape):
    return pl.BlockSpec(shape, lambda *a: (0,) * len(shape))


def lane_sums(group, acc_ref):
    return [
        [
            jnp.sum(jnp.transpose(acc_ref[k, g * BS : (g + 1) * BS, :]), axis=0, keepdims=True)
            for g in range(group)
        ]
        for k in range(3)
    ]


def phi_block(g, base, reach, idx_ref, cols_ref, ctl_ref, tile_ref):
    for lo in range(0, BS, CHUNK):
        own = [
            jnp.broadcast_to(cols_ref[g, lo : lo + CHUNK, k : k + 1], (CHUNK, BS)) for k in range(3)
        ]
        for t in range(reach):
            at = idx_ref[base + t]
            dist = None
            for k in range(3):
                gap = own[k] - ctl_ref[pl.ds(at + 64 * k, 1), :]
                dist = gap * gap if dist is None else dist + gap * gap
            ratio = dist * lax.rsqrt(jnp.maximum(dist, 1e-30))
            inner = jnp.maximum(1.0 - ratio, 0.0)
            sq = inner * inner
            tile_ref[g * reach + t, lo : lo + CHUNK, :] = (sq * sq) * (4.0 * ratio + 1.0)


def tiles_kernel(reach, group, idx_ref, pts_ref, ctl_ref, tile_ref, cols_ref):
    step = pl.program_id(0)
    for g in range(group):
        cols_ref[g] = jnp.transpose(pts_ref[g])

    def one(g, carry):
        phi_block(g, (step * group + g) * reach, reach, idx_ref, cols_ref, ctl_ref, tile_ref)
        return carry

    lax.fori_loop(0, group, one, 0)


def make_tiles(idx, pts, ctl, reach, group):
    count = pts.shape[0]
    in_specs = [pl.BlockSpec((group, 8, BS), lambda m, *_: (m, 0, 0)), whole(ctl.shape)]
    elements = count * reach * BS * BS
    return pl.pallas_call(
        functools.partial(tiles_kernel, reach, group),
        out_shape=jax.ShapeDtypeStruct((count * reach, BS, BS), jnp.float32),
        grid_spec=pltpu.PrefetchScalarGridSpec(
            num_scalar_prefetch=1,
            grid=(count // group,),
            in_specs=in_specs,
            out_specs=pl.BlockSpec((group * reach, BS, BS), lambda m, *_: (m, 0, 0)),
            scratch_shapes=[pltpu.VMEM((group, BS, 8), jnp.float32)],
        ),
        compiler_params=pltpu.CompilerParams(vmem_limit_bytes=VMEM),
        cost_estimate=pl.CostEstimate(
            flops=elements * 24, bytes_accessed=elements * 4, transcendentals=elements
        ),
    )(idx, pts, ctl)


def node_kernel(
    reach, stored, fresh, total, idx_ref, at_ref, tile_ref, f_ref, p_ref, pts_ref, ctl_ref,
    sum_ref, more_ref, new_ref, cols_ref, rows_ref, raw_ref,
):
    step = pl.program_id(0)
    for g in range(fresh):
        cols_ref[g] = jnp.transpose(pts_ref[g])
    rows_ref[...] = jnp.zeros_like(rows_ref)

    def first(g):
        return jnp.where(g < stored, step * stored + g, total + step * fresh + g - stored) * reach

    def fill(g, carry):
        base = first(g)
        for t in range(reach):
            at = idx_ref[base + t]
            for k in range(3):
                rows_ref[g, k : k + 1, t * BS : (t + 1) * BS] = f_ref[pl.ds(at + 16 * k, 1), :]
                rows_ref[g, k + 3 : k + 4, t * BS : (t + 1) * BS] = p_ref[pl.ds(at + 16 * k, 1), :]
        return carry

    lax.fori_loop(0, stored + fresh, fill, 0)

    def apply(src_ref, g, slot):
        rows = rows_ref[slot]
        high = rows.astype(jnp.bfloat16).astype(jnp.float32)
        cut = jnp.concatenate([high, rows - high], axis=0).astype(jnp.bfloat16)
        tile = jnp.concatenate([src_ref[g * reach + t] for t in range(reach)], axis=1)
        high = tile.astype(jnp.bfloat16)
        rest = (tile - high.astype(jnp.float32)).astype(jnp.bfloat16)
        dims = (((1,), (1,)), ((), ()))
        out = lax.dot_general(high, cut, dims, preferred_element_type=jnp.float32)
        raw_ref[slot] = out + lax.dot_general(rest, cut, dims, preferred_element_type=jnp.float32)

    def old(g, carry):
        apply(tile_ref, g, g)
        return carry

    def make(g, carry):
        phi_block(
            g, (total + step * fresh + g) * reach, reach, at_ref, cols_ref, ctl_ref, new_ref
        )
        return carry

    lax.fori_loop(0, stored, old, 0, unroll=UNROLL)
    if fresh:
        lax.fori_loop(0, fresh, make, 0)
        for g in range(fresh):
            apply(new_ref, g, stored + g)
    for g in range(stored + fresh):
        both = jnp.transpose(raw_ref[g])
        both = both[:8] + both[8:]
        if g < stored:
            sum_ref[g] = both
        else:
            more_ref[g - stored] = both


def node_sums(idx, at, tiles, f, p, pts, ctl, reach, steps):
    total, extra = tiles.shape[0] // reach, pts.shape[0]
    stored, fresh = total // steps, extra // steps
    elements = (total + extra) * reach * BS * BS

    def block(count):
        return pl.BlockSpec((count, 8, BS), lambda m, *_: (m, 0, 0))

    return pl.pallas_call(
        functools.partial(node_kernel, reach, stored, fresh, total),
        out_shape=[
            jax.ShapeDtypeStruct((total, 8, BS), jnp.float32),
            jax.ShapeDtypeStruct((extra, 8, BS), jnp.float32),
        ],
        grid_spec=pltpu.PrefetchScalarGridSpec(
            num_scalar_prefetch=2,
            grid=(steps,),
            in_specs=[
                pl.BlockSpec((stored * reach, BS, BS), lambda m, *_: (m, 0, 0)),
                whole(f.shape),
                whole(p.shape),
                block(fresh),
                whole(ctl.shape),
            ],
            out_specs=[block(stored), block(fresh)],
            scratch_shapes=[
                pltpu.VMEM((fresh * reach, BS, BS), jnp.float32),
                pltpu.VMEM((fresh, BS, 8), jnp.float32),
                pltpu.VMEM((stored + fresh, 8, reach * BS), jnp.float32),
                pltpu.VMEM((stored + fresh, BS, 16), jnp.float32),
            ],
        ),
        compiler_params=pltpu.CompilerParams(vmem_limit_bytes=VMEM),
        cost_estimate=pl.CostEstimate(
            flops=elements * 12, bytes_accessed=elements * 4, transcendentals=0
        ),
    )(idx, at, tiles, f, p, pts, ctl)


def operator_sums(tile_ref, acc_ref, row):
    def one(g, carry):
        start = pl.multiple_of(g * BS, BS)
        for lo in range(0, BS, CHUNK):
            acc = [jnp.zeros((CHUNK, BS), jnp.float32) for _ in range(3)]
            for t in range(9):
                tile = tile_ref[g * 9 + t, lo : lo + CHUNK, :]
                for k in range(3):
                    part = row(g * 9 + t, k)
                    acc[k] = acc[k] + tile * (part * 8.0 if t == 0 else part)
            for k in range(3):
                acc_ref[k, pl.ds(start + lo, CHUNK), :] = acc[k]
        return carry

    lax.fori_loop(0, 16, one, 0)
    return lane_sums(16, acc_ref)


OPERATOR_SCRATCH = [
    pltpu.VMEM((144, BS, BS), jnp.float32),
    pltpu.VMEM((3, 16 * BS, BS), jnp.float32),
    pltpu.SemaphoreType.DMA,
]


def spread_kernel(
    idx_ref, want_ref, pts_ref, half_hbm, other_hbm, sens_hbm,
    own_ref, image_ref, tile_hbm, ctl_hbm,
    near_ref, sens_ref, ctl_ref, cols_ref, half_sem, tile_sem, tile_ref, acc_ref, sem,
):
    size = half_hbm.shape[0]
    first = pltpu.make_async_copy(half_hbm, ctl_ref.at[pl.ds(0, size), :], half_sem.at[0])
    second = pltpu.make_async_copy(other_hbm, ctl_ref.at[pl.ds(size, size), :], half_sem.at[1])
    sens_copy = pltpu.make_async_copy(sens_hbm, sens_ref, sem)
    ctl_copy = pltpu.make_async_copy(ctl_ref, ctl_hbm, half_sem.at[2])
    first.start()
    second.start()
    sens_copy.start()
    for g in range(16):
        cols_ref[g] = jnp.transpose(pts_ref[g])
    first.wait()
    second.wait()
    ctl_copy.start()

    def tile_copy(g):
        rows = pl.ds(g * 9, 9)
        return pltpu.make_async_copy(tile_ref.at[rows], tile_hbm.at[rows], tile_sem.at[g])

    def make(g, carry):
        phi_block(g, g * 9, 9, idx_ref, cols_ref, ctl_ref, tile_ref)
        tile_copy(g).start()
        return carry

    lax.fori_loop(0, 16, make, 0)
    sens_copy.wait()
    ids = jnp.sum(sens_ref[:, 48, :].reshape(16, 8, BS), axis=1)
    want = want_ref[...]
    acc = [jnp.zeros((144, BS), jnp.float32) for _ in range(3)]
    for g in range(16):
        hot = (want == ids[g : g + 1, :]).astype(jnp.bfloat16)
        for k in range(3):
            part = sens_ref[8 * g : 8 * g + 8, 16 * k : 16 * k + 16, :].reshape(BS, BS)
            high = part.astype(jnp.bfloat16)
            rest = (part - high.astype(jnp.float32)).astype(jnp.bfloat16)
            acc[k] = acc[k] + jnp.dot(hot, high, preferred_element_type=jnp.float32)
            acc[k] = acc[k] + jnp.dot(hot, rest, preferred_element_type=jnp.float32)
    for k in range(3):
        near_ref[144 * k : 144 * k + 144] = acc[k]
    sums = operator_sums(tile_ref, acc_ref, lambda n, k: near_ref[pl.ds(n + 144 * k, 1), :])
    for k in range(3):
        for g in range(16):
            own = near_ref[144 * k + 9 * g : 144 * k + 9 * g + 1, :]
            own_ref[16 * k + g : 16 * k + g + 1, :] = own
            image_ref[0, 16 * k + g : 16 * k + g + 1, :] = own + sums[k][g] * COUPLING
    for n in range(1, 16):
        image_ref[n] = image_ref[0]
    ctl_copy.wait()
    for g in range(16):
        tile_copy(g).wait()


def spread_and_apply(idx, want, pts, half, other, sens):
    vmem, hbm = pl.BlockSpec(memory_space=pltpu.VMEM), pl.BlockSpec(memory_space=pl.ANY)
    tiles = (144, BS, BS)
    coords = (2 * half.shape[0], BS)
    return pl.pallas_call(
        spread_kernel,
        out_shape=[
            jax.ShapeDtypeStruct((48, BS), jnp.float32),
            jax.ShapeDtypeStruct((16, 48, BS), jnp.float32),
            jax.ShapeDtypeStruct(tiles, jnp.float32),
            jax.ShapeDtypeStruct(coords, jnp.float32),
        ],
        in_specs=[pl.BlockSpec(memory_space=pltpu.SMEM), vmem, vmem, hbm, hbm, hbm],
        out_specs=[vmem, vmem, hbm, hbm],
        scratch_shapes=[
            pltpu.VMEM((3 * 144, BS), jnp.float32),
            pltpu.VMEM(sens.shape, jnp.float32),
            pltpu.VMEM(coords, jnp.float32),
            pltpu.VMEM((16, BS, 8), jnp.float32),
            pltpu.SemaphoreType.DMA((3,)),
            pltpu.SemaphoreType.DMA((16,)),
        ]
        + OPERATOR_SCRATCH,
        compiler_params=pltpu.CompilerParams(vmem_limit_bytes=VMEM),
        cost_estimate=pl.CostEstimate(
            flops=144 * 2048 * 384 * 4, bytes_accessed=144 * BS * BS * 4, transcendentals=0
        ),
    )(idx, want, pts, half, other, sens)


def spread_all_kernel(sens_ref, out_ref, cut_ref, ids_ref):
    step = pl.program_id(0)

    @pl.when(step == 0)
    def _():
        ids_ref[...] = jnp.sum(sens_ref[:, 48, :].reshape(16, 8, BS), axis=1)
        for k in range(3):
            part = sens_ref[:, 16 * k : 16 * k + 16, :].reshape(2048, BS)
            high = part.astype(jnp.bfloat16)
            cut_ref[:, k * BS : (k + 1) * BS] = high
            cut_ref[:, (k + 3) * BS : (k + 4) * BS] = (part - high.astype(jnp.float32)).astype(jnp.bfloat16)

    want = (lax.broadcasted_iota(jnp.int32, (256, BS), 0) + step * 256).astype(jnp.float32)
    hot = jnp.concatenate(
        [(want == ids_ref[g : g + 1, :]).astype(jnp.bfloat16) for g in range(16)], axis=1
    )
    acc = jnp.dot(hot, cut_ref[...], preferred_element_type=jnp.float32)
    acc = acc[:, : 3 * BS] + acc[:, 3 * BS :]
    for k in range(3):
        out_ref[:, 16 * k : 16 * k + 16, :] = acc[:, k * BS : (k + 1) * BS].reshape(16, 16, BS)


def spread_all(sens):
    return pl.pallas_call(
        spread_all_kernel,
        out_shape=jax.ShapeDtypeStruct((128, 48, BS), jnp.float32),
        grid=(8,),
        in_specs=[whole(sens.shape)],
        out_specs=pl.BlockSpec((16, 48, BS), lambda m: (m, 0, 0)),
        scratch_shapes=[
            pltpu.VMEM((2048, 6 * BS), jnp.bfloat16),
            pltpu.VMEM((16, BS), jnp.float32),
        ],
        compiler_params=pltpu.CompilerParams(vmem_limit_bytes=VMEM),
        cost_estimate=pl.CostEstimate(
            flops=2048 * 2048 * 384 * 4, bytes_accessed=sens.size * 8, transcendentals=0
        ),
    )(sens)


def total_of(part):
    return jnp.sum(jnp.sum(part, axis=0, keepdims=True), axis=1, keepdims=True)


def step_kernel(idx_ref, f_ref, q_ref, tile_hbm, p_ref, coef_ref, dot_ref, tile_ref, acc_ref, sem):
    copy = pltpu.make_async_copy(tile_hbm, tile_ref, sem)
    copy.start()
    zeros = tuple(jnp.zeros((16, BS), jnp.float32) for _ in range(6))

    def at(d, k):
        return pl.ds(pl.multiple_of(d * 48 + 16 * k, 16), 16)

    def first(d, carry):
        out = []
        for k in range(3):
            f, q = f_ref[at(d, k), :], q_ref[at(d, k), :]
            out += [carry[2 * k] + f * f, carry[2 * k + 1] + f * q]
        return tuple(out)

    sums = lax.fori_loop(0, 128, first, zeros, unroll=4)
    now = [total_of(sums[2 * k]) for k in range(3)]
    alpha = [now[k] / total_of(sums[2 * k + 1]) for k in range(3)]

    def second(d, carry):
        out = []
        for k in range(3):
            r = f_ref[at(d, k), :] - alpha[k] * q_ref[at(d, k), :]
            p_ref[at(d, k), :] = r
            out.append(carry[k] + r * r)
        return tuple(out)

    sums = lax.fori_loop(0, 128, second, zeros[:3], unroll=4)
    later = [total_of(sums[k]) for k in range(3)]
    beta = [later[k] / now[k] for k in range(3)]

    def third(d, carry):
        for k in range(3):
            p_ref[at(d, k), :] = p_ref[at(d, k), :] + beta[k] * f_ref[at(d, k), :]
        return carry

    lax.fori_loop(0, 128, third, 0, unroll=4)
    rows = lax.broadcasted_iota(jnp.int32, (8, BS), 0)
    out = jnp.zeros((8, BS), jnp.float32)
    for k in range(3):
        out = jnp.where(rows == k, alpha[k], out)
        out = jnp.where(rows == 4 + k, later[k], out)
    coef_ref[...] = out
    copy.wait()
    sums = operator_sums(tile_ref, acc_ref, lambda n, k: p_ref[pl.ds(idx_ref[n] + 16 * k, 1), :])
    lanes = lax.broadcasted_iota(jnp.int32, (1, BS), 1)
    out = jnp.zeros((1, BS), jnp.float32)
    for k in range(3):
        total = jnp.zeros((1, BS), jnp.float32)
        for g in range(16):
            own = p_ref[pl.ds(idx_ref[9 * g] + 16 * k, 1), :]
            total = total + own * (own + sums[k][g] * COUPLING)
        out = jnp.where(lanes == k, jnp.sum(total, axis=1, keepdims=True), out)
    dot_ref[...] = jnp.broadcast_to(out[None], (128, 8, BS))


def step_and_apply(idx, f, q, tiles):
    vmem = pl.BlockSpec(memory_space=pltpu.VMEM)
    return pl.pallas_call(
        step_kernel,
        out_shape=[
            jax.ShapeDtypeStruct(f.shape, jnp.float32),
            jax.ShapeDtypeStruct((8, BS), jnp.float32),
            jax.ShapeDtypeStruct((128, 8, BS), jnp.float32),
        ],
        in_specs=[pl.BlockSpec(memory_space=pltpu.SMEM), vmem, vmem, pl.BlockSpec(memory_space=pl.ANY)],
        scratch_shapes=OPERATOR_SCRATCH,
        input_output_aliases={2: 0},
        compiler_params=pltpu.CompilerParams(vmem_limit_bytes=VMEM),
        cost_estimate=pl.CostEstimate(
            flops=f.size * 10 + tiles.size * 6, bytes_accessed=tiles.size * 8, transcendentals=0
        ),
    )(idx, f, q, tiles)


def copies(x):
    return jnp.broadcast_to(x[None], (lax.axis_size("ctl"),) + x.shape)


def over_ctl(x):
    return lax.all_to_all(x, "ctl", 0, 0, tiled=True)


def over_vol(x):
    return lax.all_gather(x, "vol", axis=0, tiled=True)


def place(block):
    return (((block >> 4) & 7) * 16 + (block >> 7)) * 48 + (block & 15)


def slot(block):
    return (((block >> 4) & 7) * 16 + (block >> 7)) * 16 + (block & 15)


def padded(rows):
    return jnp.pad(rows.transpose(1, 0, 2), ((0, 0), (0, 5), (0, 0)))


def body(sensitivity, sens_ids, ctl_coords, partners, node_coords, node_tiles):
    vol, ctl = lax.axis_index("vol"), lax.axis_index("ctl")
    device = vol * 16 + ctl
    blocks = ctl_coords.reshape(3, 128, BS)
    own_coords = lax.dynamic_slice_in_dim(blocks, vol * 16, 16, 1)
    ids = slot(sens_ids).astype(jnp.float32)
    lanes = jnp.arange(BS) // 16 == device % 8
    id_row = jnp.where(lanes, jnp.tile(ids, 8), 0.0)[None]
    payload = jnp.concatenate(
        [sensitivity.reshape(48, BS), jnp.pad(id_row, ((0, 7), (0, 0)))], axis=0
    )
    core = vol % 2
    own = ctl * 128 + vol * 16 + jnp.arange(16, dtype=jnp.int32)
    mates = lax.dynamic_slice_in_dim(partners, vol * 16, 16, 0)
    lists = jnp.concatenate([own[:, None], mates], axis=1).reshape(-1)
    node_lists = node_tiles.reshape(-1)

    def coord_at(block):
        return ((((block >> 6) & 1) ^ core) * 16 + (block >> 7)) * 192 + (block & 63)

    points = padded(node_coords.reshape(3, 64, BS))
    ready = (
        place(lists),
        place(node_lists),
        coord_at(lists),
        coord_at(node_lists),
        padded(own_coords),
        points[:STORED],
        points[STORED:],
        jnp.broadcast_to(slot(lists).astype(jnp.float32)[:, None], (144, BS)),
    )
    half = copies(lax.dynamic_slice_in_dim(blocks, core * 64, 64, 1).reshape(192, BS))
    sens = over_vol(over_ctl(copies(payload)))
    half = over_ctl(half)
    half, ready = lax.optimization_barrier((half, ready))
    op_at, node_at, op_coord_at, node_coord_at, own_points, points, more_points, want = ready
    other = lax.ppermute(half, "vol", [(i, i ^ 1) for i in range(lax.axis_size("vol"))])
    f_own, image, op_tiles, coords_rows = spread_and_apply(
        op_coord_at, want, own_points, half.reshape(-1, BS), other.reshape(-1, BS), sens
    )
    image, sens = lax.optimization_barrier((image, sens))
    near_image = over_ctl(image)
    f_all = spread_all(sens)
    near_image, f_all, coords_rows = lax.optimization_barrier((near_image, f_all, coords_rows))
    image_all = over_vol(near_image).reshape(128 * 48, BS)
    f_rows = f_all.reshape(128 * 48, BS)
    tiles = make_tiles(node_coord_at, points, coords_rows, 9, 8)
    image_all, tiles = lax.optimization_barrier((image_all, tiles))
    p_rows, coef, dot_row = step_and_apply(op_at, f_rows, image_all, op_tiles)

    def mine(full):
        part = lax.dynamic_slice_in_dim(full.reshape(8, 16, 3, 16, BS), ctl, 1, 1)
        return part.reshape(8, 3, 16, BS).transpose(1, 0, 2, 3).reshape(3, 128, BS)

    f_mine, p_mine = mine(f_rows), mine(p_rows)
    alpha0 = coef[0:3, 0]
    dot_rows, p_rows, f_mine, p_mine = lax.optimization_barrier(
        (dot_row, p_rows, f_mine, p_mine)
    )
    dot_rows = lax.all_to_all(dot_rows, ("vol", "ctl"), 0, 0, tiled=True)
    sums, more = node_sums(
        node_at, node_coord_at, tiles, f_rows, p_rows, more_points, coords_rows, 9, 8
    )
    dot_rows, sums, more = lax.optimization_barrier((dot_rows, sums, more))
    sums = jnp.concatenate([sums, more], axis=0).transpose(1, 0, 2)
    alpha1 = coef[4:7, 0] / jnp.sum(dot_rows[:, 0], axis=0)[:3]

    weights = alpha0[:, None, None] * f_mine + alpha1[:, None, None] * p_mine
    shift = NODE_SCALE * (
        alpha0[:, None, None] * sums[0:3] + alpha1[:, None, None] * sums[3:6]
    )
    return weights.reshape(3, -1), shift.reshape(3, -1)


def solution(mesh):
    placed = (
        P(None, ("vol", "ctl")),
        P(("vol", "ctl")),
        P(None, "ctl"),
        P("ctl", None),
        P(None, ("vol", "ctl")),
        P(("vol", "ctl"), None),
    )
    return jax.shard_map(
        body,
        mesh=mesh,
        in_specs=placed,
        out_specs=(P(None, "ctl"), P(None, ("vol", "ctl"))),
        check_vma=False,
    )
```

```python
import functools

import jax
import jax.numpy as jnp
from jax import lax
from jax.experimental import pallas as pl
from jax.experimental.pallas import tpu as pltpu
from jax.sharding import PartitionSpec as P

BS = 128
COUPLING = 0.0625
NODE_SCALE = 0.25
VMEM = 56 * 1024 * 1024
CHUNK = 32
STORED = 56
UNROLL = 7


def whole(shape):
    return pl.BlockSpec(shape, lambda *a: (0,) * len(shape))


def lane_sums(group, acc_ref):
    return [
        [
            jnp.sum(jnp.transpose(acc_ref[k, g * BS : (g + 1) * BS, :]), axis=0, keepdims=True)
            for g in range(group)
        ]
        for k in range(3)
    ]


def phi_block(g, base, reach, idx_ref, cols_ref, ctl_ref, tile_ref):
    for lo in range(0, BS, CHUNK):
        own = [
            jnp.broadcast_to(cols_ref[g, lo : lo + CHUNK, k : k + 1], (CHUNK, BS)) for k in range(3)
        ]
        for t in range(reach):
            at = idx_ref[base + t]
            dist = None
            for k in range(3):
                gap = own[k] - ctl_ref[pl.ds(at + 64 * k, 1), :]
                dist = gap * gap if dist is None else dist + gap * gap
            ratio = dist * lax.rsqrt(jnp.maximum(dist, 1e-30))
            inner = jnp.maximum(1.0 - ratio, 0.0)
            sq = inner * inner
            tile_ref[g * reach + t, lo : lo + CHUNK, :] = (sq * sq) * (4.0 * ratio + 1.0)


def tiles_kernel(reach, group, idx_ref, pts_ref, ctl_ref, tile_ref, cols_ref):
    step = pl.program_id(0)
    for g in range(group):
        cols_ref[g] = jnp.transpose(pts_ref[g])

    def one(g, carry):
        phi_block(g, (step * group + g) * reach, reach, idx_ref, cols_ref, ctl_ref, tile_ref)
        return carry

    lax.fori_loop(0, group, one, 0)


def make_tiles(idx, pts, ctl, reach, group):
    count = pts.shape[0]
    in_specs = [pl.BlockSpec((group, 8, BS), lambda m, *_: (m, 0, 0)), whole(ctl.shape)]
    elements = count * reach * BS * BS
    return pl.pallas_call(
        functools.partial(tiles_kernel, reach, group),
        out_shape=jax.ShapeDtypeStruct((count * reach, BS, BS), jnp.float32),
        grid_spec=pltpu.PrefetchScalarGridSpec(
            num_scalar_prefetch=1,
            grid=(count // group,),
            in_specs=in_specs,
            out_specs=pl.BlockSpec((group * reach, BS, BS), lambda m, *_: (m, 0, 0)),
            scratch_shapes=[pltpu.VMEM((group, BS, 8), jnp.float32)],
        ),
        compiler_params=pltpu.CompilerParams(vmem_limit_bytes=VMEM),
        cost_estimate=pl.CostEstimate(
            flops=elements * 24, bytes_accessed=elements * 4, transcendentals=elements
        ),
    )(idx, pts, ctl)


def node_kernel(
    reach, stored, fresh, total, idx_ref, at_ref, tile_ref, f_ref, p_ref, pts_ref, ctl_ref,
    sum_ref, more_ref, new_ref, cols_ref, rows_ref, raw_ref,
):
    step = pl.program_id(0)
    for g in range(fresh):
        cols_ref[g] = jnp.transpose(pts_ref[g])
    rows_ref[...] = jnp.zeros_like(rows_ref)

    def fill(g, base):
        for t in range(reach):
            at = idx_ref[base + t]
            for k in range(3):
                rows_ref[g, k : k + 1, t * BS : (t + 1) * BS] = f_ref[pl.ds(at + 16 * k, 1), :]
                rows_ref[g, k + 3 : k + 4, t * BS : (t + 1) * BS] = p_ref[pl.ds(at + 16 * k, 1), :]

    def apply(src_ref, g, slot):
        rows = rows_ref[slot]
        high = rows.astype(jnp.bfloat16).astype(jnp.float32)
        cut = jnp.concatenate([high, rows - high], axis=0).astype(jnp.bfloat16)
        tile = jnp.concatenate([src_ref[g * reach + t] for t in range(reach)], axis=1)
        high = tile.astype(jnp.bfloat16)
        rest = (tile - high.astype(jnp.float32)).astype(jnp.bfloat16)
        dims = (((1,), (1,)), ((), ()))
        out = lax.dot_general(high, cut, dims, preferred_element_type=jnp.float32)
        raw_ref[slot] = out + lax.dot_general(rest, cut, dims, preferred_element_type=jnp.float32)

    def old(g, carry):
        fill(g, (step * stored + g) * reach)
        apply(tile_ref, g, g)
        return carry

    def make(g, carry):
        phi_block(
            g, (total + step * fresh + g) * reach, reach, at_ref, cols_ref, ctl_ref, new_ref
        )
        return carry

    lax.fori_loop(0, stored, old, 0, unroll=UNROLL)
    if fresh:
        lax.fori_loop(0, fresh, make, 0)
        for g in range(fresh):
            fill(stored + g, (total + step * fresh + g) * reach)
            apply(new_ref, g, stored + g)
    for g in range(stored + fresh):
        both = jnp.transpose(raw_ref[g])
        both = both[:8] + both[8:]
        if g < stored:
            sum_ref[g] = both
        else:
            more_ref[g - stored] = both


def node_sums(idx, at, tiles, f, p, pts, ctl, reach, steps):
    total, extra = tiles.shape[0] // reach, pts.shape[0]
    stored, fresh = total // steps, extra // steps
    elements = (total + extra) * reach * BS * BS

    def block(count):
        return pl.BlockSpec((count, 8, BS), lambda m, *_: (m, 0, 0))

    return pl.pallas_call(
        functools.partial(node_kernel, reach, stored, fresh, total),
        out_shape=[
            jax.ShapeDtypeStruct((total, 8, BS), jnp.float32),
            jax.ShapeDtypeStruct((extra, 8, BS), jnp.float32),
        ],
        grid_spec=pltpu.PrefetchScalarGridSpec(
            num_scalar_prefetch=2,
            grid=(steps,),
            in_specs=[
                pl.BlockSpec((stored * reach, BS, BS), lambda m, *_: (m, 0, 0)),
                whole(f.shape),
                whole(p.shape),
                block(fresh),
                whole(ctl.shape),
            ],
            out_specs=[block(stored), block(fresh)],
            scratch_shapes=[
                pltpu.VMEM((fresh * reach, BS, BS), jnp.float32),
                pltpu.VMEM((fresh, BS, 8), jnp.float32),
                pltpu.VMEM((stored + fresh, 8, reach * BS), jnp.float32),
                pltpu.VMEM((stored + fresh, BS, 16), jnp.float32),
            ],
        ),
        compiler_params=pltpu.CompilerParams(vmem_limit_bytes=VMEM),
        cost_estimate=pl.CostEstimate(
            flops=elements * 12, bytes_accessed=elements * 4, transcendentals=0
        ),
    )(idx, at, tiles, f, p, pts, ctl)


def operator_sums(tile_ref, acc_ref, row):
    def one(g, carry):
        start = pl.multiple_of(g * BS, BS)
        for lo in range(0, BS, CHUNK):
            acc = [jnp.zeros((CHUNK, BS), jnp.float32) for _ in range(3)]
            for t in range(9):
                tile = tile_ref[g * 9 + t, lo : lo + CHUNK, :]
                for k in range(3):
                    part = row(g * 9 + t, k)
                    acc[k] = acc[k] + tile * (part * 8.0 if t == 0 else part)
            for k in range(3):
                acc_ref[k, pl.ds(start + lo, CHUNK), :] = acc[k]
        return carry

    lax.fori_loop(0, 16, one, 0)
    return lane_sums(16, acc_ref)


OPERATOR_SCRATCH = [
    pltpu.VMEM((144, BS, BS), jnp.float32),
    pltpu.VMEM((3, 16 * BS, BS), jnp.float32),
    pltpu.SemaphoreType.DMA,
]


def spread_kernel(
    idx_ref, want_ref, pts_ref, half_hbm, other_hbm, sens_hbm,
    own_ref, image_ref, tile_hbm, ctl_hbm,
    near_ref, sens_ref, ctl_ref, cols_ref, half_sem, tile_sem, tile_ref, acc_ref, sem,
):
    size = half_hbm.shape[0]
    first = pltpu.make_async_copy(half_hbm, ctl_ref.at[pl.ds(0, size), :], half_sem.at[0])
    second = pltpu.make_async_copy(other_hbm, ctl_ref.at[pl.ds(size, size), :], half_sem.at[1])
    sens_copy = pltpu.make_async_copy(sens_hbm, sens_ref, sem)
    ctl_copy = pltpu.make_async_copy(ctl_ref, ctl_hbm, half_sem.at[2])
    first.start()
    second.start()
    sens_copy.start()
    for g in range(16):
        cols_ref[g] = jnp.transpose(pts_ref[g])
    first.wait()
    second.wait()
    ctl_copy.start()

    def tile_copy(g):
        rows = pl.ds(g * 9, 9)
        return pltpu.make_async_copy(tile_ref.at[rows], tile_hbm.at[rows], tile_sem.at[g])

    def make(g, carry):
        phi_block(g, g * 9, 9, idx_ref, cols_ref, ctl_ref, tile_ref)
        tile_copy(g).start()
        return carry

    lax.fori_loop(0, 16, make, 0)
    sens_copy.wait()
    ids = jnp.sum(sens_ref[:, 48, :].reshape(16, 8, BS), axis=1)
    want = want_ref[...]
    acc = [jnp.zeros((144, BS), jnp.float32) for _ in range(3)]
    for g in range(16):
        hot = (want == ids[g : g + 1, :]).astype(jnp.bfloat16)
        for k in range(3):
            part = sens_ref[8 * g : 8 * g + 8, 16 * k : 16 * k + 16, :].reshape(BS, BS)
            high = part.astype(jnp.bfloat16)
            rest = (part - high.astype(jnp.float32)).astype(jnp.bfloat16)
            acc[k] = acc[k] + jnp.dot(hot, high, preferred_element_type=jnp.float32)
            acc[k] = acc[k] + jnp.dot(hot, rest, preferred_element_type=jnp.float32)
    for k in range(3):
        near_ref[144 * k : 144 * k + 144] = acc[k]
    sums = operator_sums(tile_ref, acc_ref, lambda n, k: near_ref[pl.ds(n + 144 * k, 1), :])
    for k in range(3):
        for g in range(16):
            own = near_ref[144 * k + 9 * g : 144 * k + 9 * g + 1, :]
            own_ref[16 * k + g : 16 * k + g + 1, :] = own
            image_ref[0, 16 * k + g : 16 * k + g + 1, :] = own + sums[k][g] * COUPLING
    for n in range(1, 16):
        image_ref[n] = image_ref[0]
    ctl_copy.wait()
    for g in range(16):
        tile_copy(g).wait()


def spread_and_apply(idx, want, pts, half, other, sens):
    vmem, hbm = pl.BlockSpec(memory_space=pltpu.VMEM), pl.BlockSpec(memory_space=pl.ANY)
    tiles = (144, BS, BS)
    coords = (2 * half.shape[0], BS)
    return pl.pallas_call(
        spread_kernel,
        out_shape=[
            jax.ShapeDtypeStruct((48, BS), jnp.float32),
            jax.ShapeDtypeStruct((16, 48, BS), jnp.float32),
            jax.ShapeDtypeStruct(tiles, jnp.float32),
            jax.ShapeDtypeStruct(coords, jnp.float32),
        ],
        in_specs=[pl.BlockSpec(memory_space=pltpu.SMEM), vmem, vmem, hbm, hbm, hbm],
        out_specs=[vmem, vmem, hbm, hbm],
        scratch_shapes=[
            pltpu.VMEM((3 * 144, BS), jnp.float32),
            pltpu.VMEM(sens.shape, jnp.float32),
            pltpu.VMEM(coords, jnp.float32),
            pltpu.VMEM((16, BS, 8), jnp.float32),
            pltpu.SemaphoreType.DMA((3,)),
            pltpu.SemaphoreType.DMA((16,)),
        ]
        + OPERATOR_SCRATCH,
        compiler_params=pltpu.CompilerParams(vmem_limit_bytes=VMEM),
        cost_estimate=pl.CostEstimate(
            flops=144 * 2048 * 384 * 4, bytes_accessed=144 * BS * BS * 4, transcendentals=0
        ),
    )(idx, want, pts, half, other, sens)


def spread_all_kernel(sens_ref, out_ref, cut_ref, ids_ref):
    step = pl.program_id(0)

    @pl.when(step == 0)
    def _():
        ids_ref[...] = jnp.sum(sens_ref[:, 48, :].reshape(16, 8, BS), axis=1)
        for k in range(3):
            part = sens_ref[:, 16 * k : 16 * k + 16, :].reshape(2048, BS)
            high = part.astype(jnp.bfloat16)
            cut_ref[:, k * BS : (k + 1) * BS] = high
            cut_ref[:, (k + 3) * BS : (k + 4) * BS] = (part - high.astype(jnp.float32)).astype(jnp.bfloat16)

    want = (lax.broadcasted_iota(jnp.int32, (256, BS), 0) + step * 256).astype(jnp.float32)
    hot = jnp.concatenate(
        [(want == ids_ref[g : g + 1, :]).astype(jnp.bfloat16) for g in range(16)], axis=1
    )
    acc = jnp.dot(hot, cut_ref[...], preferred_element_type=jnp.float32)
    acc = acc[:, : 3 * BS] + acc[:, 3 * BS :]
    for k in range(3):
        out_ref[:, 16 * k : 16 * k + 16, :] = acc[:, k * BS : (k + 1) * BS].reshape(16, 16, BS)


def spread_all(sens):
    return pl.pallas_call(
        spread_all_kernel,
        out_shape=jax.ShapeDtypeStruct((128, 48, BS), jnp.float32),
        grid=(8,),
        in_specs=[whole(sens.shape)],
        out_specs=pl.BlockSpec((16, 48, BS), lambda m: (m, 0, 0)),
        scratch_shapes=[
            pltpu.VMEM((2048, 6 * BS), jnp.bfloat16),
            pltpu.VMEM((16, BS), jnp.float32),
        ],
        compiler_params=pltpu.CompilerParams(vmem_limit_bytes=VMEM),
        cost_estimate=pl.CostEstimate(
            flops=2048 * 2048 * 384 * 4, bytes_accessed=sens.size * 8, transcendentals=0
        ),
    )(sens)


def total_of(part):
    return jnp.sum(jnp.sum(part, axis=0, keepdims=True), axis=1, keepdims=True)


def step_kernel(idx_ref, f_ref, q_ref, tile_hbm, p_ref, coef_ref, dot_ref, tile_ref, acc_ref, sem):
    copy = pltpu.make_async_copy(tile_hbm, tile_ref, sem)
    copy.start()
    zeros = tuple(jnp.zeros((16, BS), jnp.float32) for _ in range(6))

    def at(d, k):
        return pl.ds(pl.multiple_of(d * 48 + 16 * k, 16), 16)

    def first(d, carry):
        out = []
        for k in range(3):
            f, q = f_ref[at(d, k), :], q_ref[at(d, k), :]
            out += [carry[2 * k] + f * f, carry[2 * k + 1] + f * q]
        return tuple(out)

    sums = lax.fori_loop(0, 128, first, zeros, unroll=4)
    now = [total_of(sums[2 * k]) for k in range(3)]
    alpha = [now[k] / total_of(sums[2 * k + 1]) for k in range(3)]

    def second(d, carry):
        out = []
        for k in range(3):
            r = f_ref[at(d, k), :] - alpha[k] * q_ref[at(d, k), :]
            p_ref[at(d, k), :] = r
            out.append(carry[k] + r * r)
        return tuple(out)

    sums = lax.fori_loop(0, 128, second, zeros[:3], unroll=4)
    later = [total_of(sums[k]) for k in range(3)]
    beta = [later[k] / now[k] for k in range(3)]

    def third(d, carry):
        for k in range(3):
            p_ref[at(d, k), :] = p_ref[at(d, k), :] + beta[k] * f_ref[at(d, k), :]
        return carry

    lax.fori_loop(0, 128, third, 0, unroll=4)
    rows = lax.broadcasted_iota(jnp.int32, (8, BS), 0)
    out = jnp.zeros((8, BS), jnp.float32)
    for k in range(3):
        out = jnp.where(rows == k, alpha[k], out)
        out = jnp.where(rows == 4 + k, later[k], out)
    coef_ref[...] = out
    copy.wait()
    sums = operator_sums(tile_ref, acc_ref, lambda n, k: p_ref[pl.ds(idx_ref[n] + 16 * k, 1), :])
    lanes = lax.broadcasted_iota(jnp.int32, (1, BS), 1)
    out = jnp.zeros((1, BS), jnp.float32)
    for k in range(3):
        total = jnp.zeros((1, BS), jnp.float32)
        for g in range(16):
            own = p_ref[pl.ds(idx_ref[9 * g] + 16 * k, 1), :]
            total = total + own * (own + sums[k][g] * COUPLING)
        out = jnp.where(lanes == k, jnp.sum(total, axis=1, keepdims=True), out)
    dot_ref[...] = jnp.broadcast_to(out[None], (128, 8, BS))


def step_and_apply(idx, f, q, tiles):
    vmem = pl.BlockSpec(memory_space=pltpu.VMEM)
    return pl.pallas_call(
        step_kernel,
        out_shape=[
            jax.ShapeDtypeStruct(f.shape, jnp.float32),
            jax.ShapeDtypeStruct((8, BS), jnp.float32),
            jax.ShapeDtypeStruct((128, 8, BS), jnp.float32),
        ],
        in_specs=[pl.BlockSpec(memory_space=pltpu.SMEM), vmem, vmem, pl.BlockSpec(memory_space=pl.ANY)],
        scratch_shapes=OPERATOR_SCRATCH,
        input_output_aliases={2: 0},
        compiler_params=pltpu.CompilerParams(vmem_limit_bytes=VMEM),
        cost_estimate=pl.CostEstimate(
            flops=f.size * 10 + tiles.size * 6, bytes_accessed=tiles.size * 8, transcendentals=0
        ),
    )(idx, f, q, tiles)


def copies(x):
    return jnp.broadcast_to(x[None], (lax.axis_size("ctl"),) + x.shape)


def over_ctl(x):
    return lax.all_to_all(x, "ctl", 0, 0, tiled=True)


def over_vol(x):
    return lax.all_gather(x, "vol", axis=0, tiled=True)


def place(block):
    return (((block >> 4) & 7) * 16 + (block >> 7)) * 48 + (block & 15)


def slot(block):
    return (((block >> 4) & 7) * 16 + (block >> 7)) * 16 + (block & 15)


def padded(rows):
    return jnp.pad(rows.transpose(1, 0, 2), ((0, 0), (0, 5), (0, 0)))


def body(sensitivity, sens_ids, ctl_coords, partners, node_coords, node_tiles):
    vol, ctl = lax.axis_index("vol"), lax.axis_index("ctl")
    device = vol * 16 + ctl
    blocks = ctl_coords.reshape(3, 128, BS)
    own_coords = lax.dynamic_slice_in_dim(blocks, vol * 16, 16, 1)
    ids = slot(sens_ids).astype(jnp.float32)
    lanes = jnp.arange(BS) // 16 == device % 8
    id_row = jnp.where(lanes, jnp.tile(ids, 8), 0.0)[None]
    payload = jnp.concatenate(
        [sensitivity.reshape(48, BS), jnp.pad(id_row, ((0, 7), (0, 0)))], axis=0
    )
    core = vol % 2
    own = ctl * 128 + vol * 16 + jnp.arange(16, dtype=jnp.int32)
    mates = lax.dynamic_slice_in_dim(partners, vol * 16, 16, 0)
    lists = jnp.concatenate([own[:, None], mates], axis=1).reshape(-1)
    node_lists = node_tiles.reshape(-1)

    def coord_at(block):
        return ((((block >> 6) & 1) ^ core) * 16 + (block >> 7)) * 192 + (block & 63)

    points = padded(node_coords.reshape(3, 64, BS))
    ready = (
        place(lists),
        place(node_lists),
        coord_at(lists),
        coord_at(node_lists),
        padded(own_coords),
        points[:STORED],
        points[STORED:],
        jnp.broadcast_to(slot(lists).astype(jnp.float32)[:, None], (144, BS)),
    )
    half = copies(lax.dynamic_slice_in_dim(blocks, core * 64, 64, 1).reshape(192, BS))
    sens = over_vol(over_ctl(copies(payload)))
    half = over_ctl(half)
    half, ready = lax.optimization_barrier((half, ready))
    op_at, node_at, op_coord_at, node_coord_at, own_points, points, more_points, want = ready
    other = lax.ppermute(half, "vol", [(i, i ^ 1) for i in range(lax.axis_size("vol"))])
    f_own, image, op_tiles, coords_rows = spread_and_apply(
        op_coord_at, want, own_points, half.reshape(-1, BS), other.reshape(-1, BS), sens
    )
    image, sens = lax.optimization_barrier((image, sens))
    near_image = over_ctl(image)
    f_all = spread_all(sens)
    near_image, f_all, coords_rows = lax.optimization_barrier((near_image, f_all, coords_rows))
    image_all = over_vol(near_image).reshape(128 * 48, BS)
    f_rows = f_all.reshape(128 * 48, BS)
    tiles = make_tiles(node_coord_at, points, coords_rows, 9, 8)
    image_all, tiles = lax.optimization_barrier((image_all, tiles))
    p_rows, coef, dot_row = step_and_apply(op_at, f_rows, image_all, op_tiles)

    def mine(full):
        part = lax.dynamic_slice_in_dim(full.reshape(8, 16, 3, 16, BS), ctl, 1, 1)
        return part.reshape(8, 3, 16, BS).transpose(1, 0, 2, 3).reshape(3, 128, BS)

    f_mine, p_mine = mine(f_rows), mine(p_rows)
    alpha0 = coef[0:3, 0]
    dot_rows, p_rows, f_mine, p_mine = lax.optimization_barrier(
        (dot_row, p_rows, f_mine, p_mine)
    )
    dot_rows = lax.all_to_all(dot_rows, ("vol", "ctl"), 0, 0, tiled=True)
    sums, more = node_sums(
        node_at, node_coord_at, tiles, f_rows, p_rows, more_points, coords_rows, 9, 8
    )
    dot_rows, sums, more = lax.optimization_barrier((dot_rows, sums, more))
    sums = jnp.concatenate([sums, more], axis=0).transpose(1, 0, 2)
    alpha1 = coef[4:7, 0] / jnp.sum(dot_rows[:, 0], axis=0)[:3]

    weights = alpha0[:, None, None] * f_mine + alpha1[:, None, None] * p_mine
    shift = NODE_SCALE * (
        alpha0[:, None, None] * sums[0:3] + alpha1[:, None, None] * sums[3:6]
    )
    return weights.reshape(3, -1), shift.reshape(3, -1)


def solution(mesh):
    placed = (
        P(None, ("vol", "ctl")),
        P(("vol", "ctl")),
        P(None, "ctl"),
        P("ctl", None),
        P(None, ("vol", "ctl")),
        P(("vol", "ctl"), None),
    )
    return jax.shard_map(
        body,
        mesh=mesh,
        in_specs=placed,
        out_specs=(P(None, "ctl"), P(None, ("vol", "ctl"))),
        check_vma=False,
    )
```
